256 devices in a mesh: sub: 64 (over z, y, core), inner: 4 (over x).
Axes of the slice: x: 4, y: 4, z: 8, core: 2. Of those that a mesh axis runs over, the one named last changes fastest.
Arguments:
- solution: float32 [32, 3, 256, 16, 128], P(None, None, 'sub', 'inner'), may hold values from -6 to 6
- residual: float32 [32, 3, 256, 16, 128], P(None, None, 'sub', 'inner'), may hold values from -6 to 6
- direction: float32 [32, 3, 256, 16, 128], P(None, None, 'sub', 'inner'), may hold values from -6 to 6
- mass: float32 [256, 16, 128], P('sub', 'inner'), may hold values from 0.2 to 5
- coarse_basis: float32 [32, 3, 256, 16, 128], P(None, None, 'sub', 'inner'), may hold values from -1 to 1
- line_inverse: float32 [64, 4, 128, 128], P('sub', 'inner'), may hold values from -1.5 to 1.5
- coarse_factor: float32 [8192, 8192], P(('sub', 'inner')), may hold values from -1 to 1
Outputs:
- new_solution: float32 [32, 3, 256, 16, 128], P(None, None, 'sub', 'inner')
- new_residual: float32 [32, 3, 256, 16, 128], P(None, None, 'sub', 'inner')
- new_direction: float32 [32, 3, 256, 16, 128], P(None, None, 'sub', 'inner')
The draws below stay inside these ranges and needn't reach their ends.
All inputs are finite; a program needn't handle non-finite values.
Results may differ from the reference program's by a relative error of at most 0.00017.
Values sent between devices are 32-bit elements; how exact they have to be, the bound alone decides.
No kernel may reach another device: no remote copies, remote signals or barrier semaphores. Data moves between devices by JAX's collectives and lax.ppermute only.
A program may use at most 64 MiB of HBM per device.

```python
import math
import jax
import jax.numpy as jnp
from jax import lax

K = 32
NB = 32
CX = 4
CY = 4
CZ = 128
NX = 256
NY = 16
NZ = 128
NCOARSE = 8192
N_SUB = 64
N_INNER = 4


def paired_fields(key):
    first = jax.random.fold_in(key, 31)
    second = jax.random.fold_in(key, 32)
    shape = (K, 3, NX, NY, NZ)
    base = jnp.clip(jax.random.normal(first, shape, jnp.float32), -6.0, 6.0)
    noise = jnp.clip(jax.random.normal(second, shape, jnp.float32), -4.0, 4.0)
    moved = jnp.clip(base + 0.3 * noise, -6.0, 6.0)
    return (base, moved)


def draw_residual(key, part):
    return paired_fields(key)[0]


def draw_direction(key, part):
    return paired_fields(key)[1]


def draw_coarse_basis(key, part):
    return jax.random.uniform(key, (NB, 3, NX, NY, NZ), jnp.float32, -1.0, 1.0)


def draw_line_inverse(key, part):
    first = jax.random.fold_in(key, 11)
    second = jax.random.fold_in(key, 12)
    diagonal = jax.random.uniform(first, (N_SUB, N_INNER, CZ), jnp.float32, 0.5, 1.5)
    noise = jnp.clip(jax.random.normal(second, (N_SUB, N_INNER, CZ, CZ), jnp.float32), -4.0, 4.0)
    symmetric = (noise + jnp.swapaxes(noise, 2, 3)) * (0.35 / CZ ** 0.5)
    eye = jnp.eye(CZ, dtype=jnp.float32)
    return symmetric * (1.0 - eye) + diagonal[..., None] * eye


def draw_coarse_factor(key, part):
    first = jax.random.fold_in(key, 21)
    second = jax.random.fold_in(key, 22)
    factor = 0.7 * (3.0 * CX * CY * CZ * NB) ** (-0.25)
    diagonal = jax.random.uniform(first, (NCOARSE,), jnp.float32, 0.5, 1.5)
    noise = jnp.clip(jax.random.normal(second, (NCOARSE, NCOARSE), jnp.float32), -4.0, 4.0)
    eye = jnp.eye(NCOARSE, dtype=jnp.float32)
    matrix = noise * (0.5 / NCOARSE ** 0.5) * (1.0 - eye) + diagonal[:, None] * eye
    return matrix * factor


def levels(own_key, dims, cuts, smallest, high):
    gain = 1.0
    for dim, parts in cuts:
        heights = jax.random.uniform(jax.random.fold_in(jax.random.fold_in(own_key, 6), dim), (parts,), jnp.float32, smallest / len(cuts), high / len(cuts))
        gain = gain * jnp.repeat(jnp.exp(heights), dims[dim] // parts).reshape((-1,) + (1,) * (len(dims) - 1 - dim))
    return gain


def scatter_about(stream_key, shape, deviation, most, split=(), held_as=jnp.bfloat16):
    entries = jax.random.normal(stream_key, shape, jnp.float32) * deviation
    if len(split) > 0:
        entries = levels(stream_key, shape, split, -0.22, 0.18) * entries
    return jnp.clip(entries, min=-most, max=most).astype(held_as)


def setup_inputs(seed: int = 0) -> dict:
    key_of = jax.random.split(jax.random.key(seed), 8)
    solution = scatter_about(key_of[0], (K, 3, NX, NY, NZ), 1.0, 6.0, ((2, 64), (3, 4)), jnp.float32)
    residual = draw_residual(jax.random.fold_in(key_of[7], 71), 0)
    direction = draw_direction(jax.random.fold_in(key_of[7], 71), 0)
    mass = jnp.clip(jnp.exp(math.log(5.0) - 3.218876 * jax.random.uniform(key_of[3], (NX, NY, NZ), jnp.float32) ** levels(key_of[3], (NX, NY, NZ), ((0, 64), (1, 4)), -0.2, 0.2)), 0.2, 5.0)
    coarse_basis = draw_coarse_basis(jax.random.fold_in(key_of[7], 71), 0)
    line_inverse = draw_line_inverse(jax.random.fold_in(key_of[7], 71), 0)
    coarse_factor = draw_coarse_factor(jax.random.fold_in(key_of[7], 71), 0)
    return {"solution": solution, "residual": residual, "direction": direction, "mass": mass, "coarse_basis": coarse_basis, "line_inverse": line_inverse, "coarse_factor": coarse_factor}


exact_mode = lax.Precision.HIGHEST

def shifted(padded, which, offset):
    window = [slice(None), slice(None)]
    for place in (2, 3, 4):
        length = padded.shape[place]
        if place == which:
            window.append(slice(2 + offset, length - 2 + offset))
        else:
            window.append(slice(2, length - 2))
    return padded[tuple(window)]

def apply_operator(padded, mass):
    center = shifted(padded, 2, 0)
    nearby = jnp.zeros_like(center)
    farther = jnp.zeros_like(center)
    for which in (2, 3, 4):
        nearby = nearby + shifted(padded, which, 1) + shifted(padded, which, -1)
        farther = farther + shifted(padded, which, 2) + shifted(padded, which, -2)
    return (mass + 7.5) * center - 4.0 / 3.0 * nearby + 1.0 / 12.0 * farther

def spd_solve(matrix, rhs):
    lower = jnp.linalg.cholesky(matrix)
    middle = lax.linalg.triangular_solve(lower, rhs, left_side=True, lower=True)
    return lax.linalg.triangular_solve(lower, middle, left_side=True, lower=True, transpose_a=True)

def reference(solution, residual, direction, mass, coarse_basis, line_inverse, coarse_factor):
    directions = direction.shape[0]
    shape = direction.shape
    padded = jnp.pad(direction, ((0, 0), (0, 0), (2, 2), (2, 2), (2, 2)))
    image = apply_operator(padded, mass)
    flat_p = direction.reshape(directions, -1)
    flat_q = image.reshape(directions, -1)
    flat_r = residual.reshape(directions, -1)
    gram_pq = jnp.dot(flat_p, flat_q.T, precision=exact_mode)
    proj_pr = jnp.dot(flat_p, flat_r.T, precision=exact_mode)
    alpha_mix = spd_solve(gram_pq, proj_pr)
    new_solution = solution + jnp.dot(alpha_mix.T, flat_p, precision=exact_mode).reshape(shape)
    flat_new = flat_r - jnp.dot(alpha_mix.T, flat_q, precision=exact_mode)
    new_residual = flat_new.reshape(shape)
    blocked = new_residual.reshape(directions, 3, N_SUB, CX, N_INNER, CY, NZ)
    basis_blocked = coarse_basis.reshape(NB, 3, N_SUB, CX, N_INNER, CY, NZ)
    local_part = jnp.einsum('abzw,kcaxbyw->kcaxbyz', line_inverse, blocked, precision=exact_mode)
    coarse_rhs = jnp.einsum('jcaxbyz,kcaxbyz->abjk', basis_blocked, blocked, precision=exact_mode)
    coarse_rhs = coarse_rhs.reshape(NB * N_SUB * N_INNER, directions)
    coarse_mid = jnp.dot(coarse_factor.T, coarse_rhs, precision=exact_mode)
    coarse_sol = jnp.dot(coarse_factor, coarse_mid, precision=exact_mode)
    coarse_sol = coarse_sol.reshape(N_SUB, N_INNER, NB, directions)
    correction = jnp.einsum('jcaxbyz,abjk->kcaxbyz', basis_blocked, coarse_sol, precision=exact_mode)
    precond = (local_part + correction).reshape(directions, -1)
    cross_qz = jnp.dot(flat_q, precond.T, precision=exact_mode)
    beta_mix = -spd_solve(gram_pq, cross_qz)
    new_direction = (precond + jnp.dot(beta_mix.T, flat_p, precision=exact_mode)).reshape(shape)
    return (new_solution, new_residual, new_direction)
```

```python
import jax
import jax.numpy as jnp
from jax import lax
from jax.experimental import pallas as pl
from jax.experimental.pallas import tpu as pltpu
from jax.sharding import Mesh
from jax.sharding import PartitionSpec as P

SUB = ("z", "y", "core")
ROWS = ("y", "x")
COLS = ("z", "core")
exact = lax.Precision.HIGHEST

K = 32
F = 48
LANES = 128


def dot(a, b, dims=((1,), (0,))):
    return lax.dot_general(a, b, (dims, ((), ())), precision=exact, preferred_element_type=jnp.float32)


def line(ref, f):
    return ref[pl.ds(f, K, stride=F), :]


def place(c, x, y):
    return (c * 4 + x) * 4 + y


def wide(ref):
    return jnp.concatenate([line(ref, f) for f in range(F)], axis=1)


def narrow(value, ref):
    for f in range(F):
        ref[pl.ds(f, K, stride=F), :] = value[:, f * LANES : (f + 1) * LANES]


def call(kernel, outs, scratch=(), flops=10_000_000, name=None):
    vmem = pl.BlockSpec(memory_space=pltpu.VMEM)

    def run(*args):
        moved = 4 * (sum(a.size for a in args) + sum(o[0] * o[1] if len(o) == 2 else o[0] * o[1] * o[2] for o in outs))
        return pl.pallas_call(
            kernel,
            out_shape=[jax.ShapeDtypeStruct(o, jnp.float32) for o in outs],
            in_specs=[vmem] * len(args),
            out_specs=[vmem] * len(outs),
            scratch_shapes=list(scratch),
            compiler_params=pltpu.CompilerParams(vmem_limit_bytes=40 * 1024 * 1024),
            cost_estimate=pl.CostEstimate(flops=flops, bytes_accessed=moved, transcendentals=0),
            name=name,
        )(*args)

    return run


def slab_kernel(p, low_x, high_x, low_y, high_y):
    at = 0
    for c in range(3):
        for x in range(2):
            for y in range(4):
                low_x[pl.ds(at * K, K), :] = line(p, place(c, x, y))
                high_x[pl.ds(at * K, K), :] = line(p, place(c, x + 2, y))
                at += 1
    at = 0
    for c in range(3):
        for x in range(4):
            for y in range(2):
                low_y[pl.ds(at * K, K), :] = line(p, place(c, x, y))
                high_y[pl.ds(at * K, K), :] = line(p, place(c, x, y + 2))
                at += 1


def lined_kernel(r, inverse, lined_r):
    lined_r[...] = dot(r[...], inverse[...], ((1,), (1,)))


def image_kernel(p, r, basis, mass, below_x, above_x, below_y, above_y, q, sums, left, right):
    lane = lax.broadcasted_iota(jnp.int32, (K, LANES), 1)

    def at(c, x, y):
        if x < 0:
            return below_x[pl.ds(((c * 2 + x + 2) * 4 + y) * K, K), :]
        if x > 3:
            return above_x[pl.ds(((c * 2 + x - 4) * 4 + y) * K, K), :]
        if y < 0:
            return below_y[pl.ds(((c * 4 + x) * 2 + y + 2) * K, K), :]
        if y > 3:
            return above_y[pl.ds(((c * 4 + x) * 2 + y - 4) * K, K), :]
        return left[pl.ds(0, K), pl.ds(place(c, x, y) * LANES, LANES)]

    for f in range(F):
        columns = pl.ds(f * LANES, LANES)
        left[pl.ds(0, K), columns] = line(p, f)
        left[pl.ds(K, K), columns] = line(basis, f)
        right[pl.ds(K, K), columns] = line(r, f)
    for c in range(3):
        for x in range(4):
            for y in range(4):
                f = place(c, x, y)
                center = at(c, x, y)
                near = at(c, x - 1, y) + at(c, x + 1, y) + at(c, x, y - 1) + at(c, x, y + 1)
                far = at(c, x - 2, y) + at(c, x + 2, y) + at(c, x, y - 2) + at(c, x, y + 2)
                near = near + jnp.where(lane >= 1, pltpu.roll(center, 1, 1), 0.0)
                near = near + jnp.where(lane < LANES - 1, pltpu.roll(center, LANES - 1, 1), 0.0)
                far = far + jnp.where(lane >= 2, pltpu.roll(center, 2, 1), 0.0)
                far = far + jnp.where(lane < LANES - 2, pltpu.roll(center, LANES - 2, 1), 0.0)
                weight = mass[pl.ds(x * 4 + y, 1), :] + 7.5
                value = weight * center - (4.0 / 3.0) * near + (1.0 / 12.0) * far
                right[pl.ds(0, K), pl.ds(f * LANES, LANES)] = value
                q[:, pl.ds(f * LANES, LANES)] = value
    both = dot(left[...], right[...], ((1,), (1,)))
    packed = jnp.concatenate([both[:K], both[K:]], axis=1)
    for g in range(16):
        sums[g] = packed


def image_lined_kernel(q, lined_r, inverse, lined_q, inner, right):
    for f in range(F):
        columns = pl.ds(f * LANES, LANES)
        right[pl.ds(f * K, K), :] = q[:, columns]
    right[...] = dot(right[...], inverse[...], ((1,), (1,)))
    for f in range(F):
        columns = pl.ds(f * LANES, LANES)
        lined_q[pl.ds(0, K), columns] = right[pl.ds(f * K, K), :]
        lined_q[pl.ds(K, K), columns] = line(lined_r, f)
    inner[...] = dot(q[...], lined_q[...], ((1,), (1,)))


def mid_kernel(gathered, factor, out):
    total = jnp.sum(gathered[...], axis=0)
    rhs = jnp.concatenate([gathered[g][:, 64:] for g in range(16)], axis=0)
    mid = dot(rhs.T, factor[...].reshape(512, 512)).T
    for g in range(16):
        out[g] = jnp.concatenate([mid[g * K : (g + 1) * K], total[:, :64]], axis=1)


def packed4(a, b):
    return jnp.concatenate([a[:16], a[16:], b[:16], b[16:]], axis=1)


def alpha_kernel(arrived, inner, alpha, lower_inverse, out):
    total = jnp.sum(arrived[...], axis=0)
    mid_q, mid_r = total[:, :32], total[:, 32:64]
    gram, proj = total[:, 64:96], total[:, 96:]
    row = lax.broadcasted_iota(jnp.int32, (K, K), 0)
    column = lax.broadcasted_iota(jnp.int32, (K, K), 1)
    eye = (row == column).astype(jnp.float32)
    work = jnp.concatenate([gram, eye], axis=1)
    below = lax.broadcasted_iota(jnp.int32, (K, 1), 0)
    scale = jnp.zeros((K, 1), jnp.float32)
    for j in range(K):
        pivot = work[j : j + 1, j : j + 1]
        factor = jnp.where(below > j, work[:, j : j + 1] / pivot, 0.0)
        scale = jnp.where(below == j, lax.rsqrt(pivot), scale)
        work = work - factor * work[j : j + 1, :]
    inverse = work[:, K:] * scale
    mix = dot(inverse, dot(inverse, proj), ((0,), (0,)))
    alpha[...] = mix
    lower_inverse[...] = inverse
    coarse_mid = mid_r - dot(mid_q, mix)
    cross = inner[:, K:] - dot(inner[:, :K], mix) + dot(mid_q, coarse_mid, ((0,), (0,)))
    packed = packed4(coarse_mid, cross)
    for g in range(16):
        out[g] = packed


def sol_kernel(gathered, factor, out):
    cross = jnp.sum(gathered[...], axis=0)[:, 64:]
    mid = jnp.concatenate([gathered[g][:, h : h + K] for g in range(16) for h in (0, K)], axis=0)
    sol = dot(factor[...].reshape(512, 512), mid)
    for g in range(16):
        at = g * K
        out[g] = jnp.concatenate([sol[at : at + 16], sol[at + 16 : at + K], cross], axis=1)


def update_kernel(s, p, r, q, lined, alpha, new_s, new_r, local):
    mix = alpha[...]
    narrow(wide(s) + dot(mix, wide(p), ((0,), (0,))), new_s)
    narrow(wide(r) - dot(mix, q[...], ((0,), (0,))), new_r)
    local[...] = lined[pl.ds(K, K), :] - dot(mix, lined[pl.ds(0, K), :], ((0,), (0,)))


def direction_kernel(arrived, lower_inverse, local, basis, p, new_p, both):
    total = jnp.sum(arrived[...], axis=0)
    sol = jnp.concatenate([total[:, :32], total[:, 32:64]], axis=0)
    cross = jnp.concatenate([total[:, 64:96], total[:, 96:]], axis=0)
    inverse = lower_inverse[...]
    beta = -dot(inverse, dot(inverse, cross), ((0,), (0,)))
    mix = jnp.concatenate([sol, beta], axis=0)
    for f in range(F):
        columns = pl.ds(f * LANES, LANES)
        both[pl.ds(0, K), columns] = line(basis, f)
        both[pl.ds(K, K), columns] = line(p, f)
    narrow(local[...] + dot(mix, both[...], ((0,), (0,))), new_p)


def swapped(array, axes):
    return lax.all_to_all(array, axes, 0, 0, tiled=True)


def on_device(solution, residual, direction, mass, coarse_basis, line_inverse, coarse_factor):
    shape = direction.shape
    s, r, p, basis = (a.reshape(-1, LANES) for a in (solution, residual, direction, coarse_basis))
    inverse = line_inverse[0, 0]
    rows, length = p.shape
    flat = (K, F * LANES)

    slabs = call(slab_kernel, [(rows // 2, LANES)] * 4, name="halo_slabs")(p)
    low_x, high_x, low_y, high_y = slabs
    up_sub = [(i, i + 1) for i in range(63)]
    up_inner = [(i, i + 1) for i in range(3)]
    below_y = lax.ppermute(high_y, "x", up_inner)
    above_y = lax.ppermute(low_y, "x", [(b, a) for a, b in up_inner])
    below_x = lax.ppermute(high_x, SUB, up_sub)
    above_x = lax.ppermute(low_x, SUB, [(b, a) for a, b in up_sub])

    blocks = jnp.swapaxes(coarse_factor.reshape(32, 16, 512), 0, 1)
    factor = swapped(blocks, ROWS)
    (lined_r,) = call(lined_kernel, [(rows, LANES)], flops=50_000_000, name="lined_residual")(r, inverse)

    q, sums = call(
        image_kernel,
        [flat, (16, K, LANES)],
        [pltpu.VMEM((2 * K, F * LANES), jnp.float32)] * 2,
        name="image",
    )(p, r, basis, mass.reshape(16, LANES), below_x, above_x, below_y, above_y)
    gathered = swapped(sums, ROWS)
    lined, inner = call(
        image_lined_kernel,
        [(2 * K, F * LANES), (K, 2 * K)],
        [pltpu.VMEM((rows, LANES), jnp.float32)],
        flops=50_000_000,
        name="lined_image",
    )(q, lined_r, inverse)
    (parts,) = call(mid_kernel, [(16, K, LANES)], name="coarse_mid")(gathered, factor)
    arrived = swapped(parts, COLS)
    alpha, lower_inverse, spread = call(alpha_kernel, [(K, K), (K, K), (16, 16, LANES)], name="alpha")(arrived, inner)
    mids = swapped(spread, COLS)
    new_s, new_r, local = call(update_kernel, [(rows, LANES)] * 2 + [flat], flops=50_000_000, name="updates")(
        s, p, r, q, lined, alpha
    )
    (sols,) = call(sol_kernel, [(16, 16, LANES)], name="coarse_sol")(mids, factor)
    last = swapped(sols, ROWS)
    (new_p,) = call(
        direction_kernel, [(rows, LANES)], [pltpu.VMEM((2 * K, F * LANES), jnp.float32)], name="new_direction"
    )(last, lower_inverse, local, basis, p)
    return new_s.reshape(shape), new_r.reshape(shape), new_p.reshape(shape)


def solution(mesh):
    torus = Mesh(mesh.devices.reshape(8, 4, 2, 4), ("z", "y", "core", "x"))
    field = P(None, None, SUB, "x", None)
    return jax.shard_map(
        on_device,
        mesh=torus,
        in_specs=(field, field, field, P(SUB, "x", None), field, P(SUB, "x", None, None), P(SUB + ("x",), None)),
        out_specs=(field, field, field),
        check_vma=False,
    )
```

```python
import jax
import jax.numpy as jnp
from jax import lax
from jax.experimental import pallas as pl
from jax.experimental.pallas import tpu as pltpu
from jax.sharding import Mesh
from jax.sharding import PartitionSpec as P

SUB = ("z", "y", "core")
ROWS = ("y", "x")
COLS = ("z", "core")
exact = lax.Precision.HIGHEST

K = 32
F = 48
LANES = 128


def dot(a, b, dims=((1,), (0,))):
    return lax.dot_general(a, b, (dims, ((), ())), precision=exact, preferred_element_type=jnp.float32)


def line(ref, f):
    return ref[pl.ds(f, K, stride=F), :]


def place(c, x, y):
    return (c * 4 + x) * 4 + y


def wide(ref):
    return jnp.concatenate([line(ref, f) for f in range(F)], axis=1)


def narrow(value, ref):
    for f in range(F):
        ref[pl.ds(f, K, stride=F), :] = value[:, f * LANES : (f + 1) * LANES]


def call(kernel, outs, fetched, stored, scratch=(), flops=10_000_000, unread=0, name=None, held=0):
    def run(*args):
        n, m = len(args), len(outs)
        whole = n - unread - fetched
        vmem, hbm = pl.BlockSpec(memory_space=pltpu.VMEM), pl.BlockSpec(memory_space=pltpu.HBM)

        def body(*refs):
            given, made, own = refs[:n], refs[n : n + m], refs[n + m :]
            buffers, semaphores = own[: fetched + stored], own[fetched + stored : 2 * (fetched + stored)]
            rest = own[2 * (fetched + stored) :]
            fetches = [
                pltpu.make_async_copy(*three) for three in zip(given[:fetched], buffers[:fetched], semaphores[:fetched])
            ]
            stores = [
                pltpu.make_async_copy(*three) for three in zip(buffers[fetched:], made[:stored], semaphores[fetched:])
            ]
            for fetch in fetches:
                fetch.start()
            kernel(
                lambda i: fetches[i].wait(),
                lambda i: stores[i].start(),
                *buffers[:fetched],
                *given[fetched : fetched + whole],
                *buffers[fetched:],
                *made[stored:],
                *rest,
            )
            for store in stores:
                store.wait()

        sizes = [a.size for a in args[: fetched + whole]]
        for o in outs:
            sizes.append(1)
            for length in o:
                sizes[-1] *= length
        return pl.pallas_call(
            body,
            out_shape=[pltpu.HBM(o, jnp.float32) for o in outs[:stored]]
            + [jax.ShapeDtypeStruct(o, jnp.float32) for o in outs[stored:]],
            in_specs=[hbm] * fetched + [vmem] * whole + [hbm] * unread,
            out_specs=[hbm] * stored + [vmem] * (m - stored),
            scratch_shapes=[pltpu.VMEM(a.shape, jnp.float32) for a in args[:fetched]]
            + [pltpu.VMEM(o, jnp.float32) for o in outs[:stored]]
            + [pltpu.SemaphoreType.DMA] * (fetched + stored)
            + [pltpu.VMEM(shape, jnp.float32) for shape in scratch],
            compiler_params=pltpu.CompilerParams(vmem_limit_bytes=24 * 1024 * 1024),
            cost_estimate=pl.CostEstimate(flops=flops, bytes_accessed=4 * sum(sizes), transcendentals=0),
            name=name,
            )(
            *(pltpu.with_memory_space_constraint(a, pltpu.HBM) for a in args[:fetched]),
            *(pltpu.with_memory_space_constraint(a, pltpu.VMEM) for a in args[fetched : fetched + held]),
            *args[fetched + held :],
        )

    return run


def slab_kernel(wait, put, p, low_x, high_x, low_y, high_y):
    wait(0)
    at = 0
    for c in range(3):
        for x in range(2):
            for y in range(4):
                low_x[pl.ds(at * K, K), :] = line(p, place(c, x, y))
                high_x[pl.ds(at * K, K), :] = line(p, place(c, x + 2, y))
                at += 1
    put(0)
    put(1)
    at = 0
    for c in range(3):
        for x in range(4):
            for y in range(2):
                low_y[pl.ds(at * K, K), :] = line(p, place(c, x, y))
                high_y[pl.ds(at * K, K), :] = line(p, place(c, x, y + 2))
                at += 1
    put(2)
    put(3)


def residual_sums_kernel(wait, put, p, basis, r, sums, left):
    wait(0)
    wait(1)
    for f in range(F):
        columns = pl.ds(f * LANES, LANES)
        left[pl.ds(0, K), columns] = line(p, f)
        left[pl.ds(K, K), columns] = line(basis, f)
    wait(2)
    sums[...] = dot(left[...], wide(r), ((1,), (1,)))


def image_kernel(wait, put, p, basis, mass, below_x, above_x, below_y, above_y, sums_r, q, sums, left):
    lane = lax.broadcasted_iota(jnp.int32, (K, LANES), 1)

    def at(c, x, y):
        if x < 0:
            return below_x[pl.ds(((c * 2 + x + 2) * 4 + y) * K, K), :]
        if x > 3:
            return above_x[pl.ds(((c * 2 + x - 4) * 4 + y) * K, K), :]
        if y < 0:
            return below_y[pl.ds(((c * 4 + x) * 2 + y + 2) * K, K), :]
        if y > 3:
            return above_y[pl.ds(((c * 4 + x) * 2 + y - 4) * K, K), :]
        return left[pl.ds(0, K), pl.ds(place(c, x, y) * LANES, LANES)]

    wait(0)
    for f in range(F):
        left[pl.ds(0, K), pl.ds(f * LANES, LANES)] = line(p, f)
    wait(2)
    for c in range(3):
        for x in range(4):
            for y in range(4):
                f = place(c, x, y)
                center = at(c, x, y)
                near = at(c, x - 1, y) + at(c, x + 1, y) + at(c, x, y - 1) + at(c, x, y + 1)
                far = at(c, x - 2, y) + at(c, x + 2, y) + at(c, x, y - 2) + at(c, x, y + 2)
                near = near + jnp.where(lane >= 1, pltpu.roll(center, 1, 1), 0.0)
                near = near + jnp.where(lane < LANES - 1, pltpu.roll(center, LANES - 1, 1), 0.0)
                far = far + jnp.where(lane >= 2, pltpu.roll(center, 2, 1), 0.0)
                far = far + jnp.where(lane < LANES - 2, pltpu.roll(center, LANES - 2, 1), 0.0)
                weight = mass[pl.ds(x * 4 + y, 1), :] + 7.5
                q[:, pl.ds(f * LANES, LANES)] = weight * center - (4.0 / 3.0) * near + (1.0 / 12.0) * far
    put(0)
    wait(1)
    for f in range(F):
        left[pl.ds(K, K), pl.ds(f * LANES, LANES)] = line(basis, f)
    sums_q = dot(left[...], q[...], ((1,), (1,)))
    packed = jnp.concatenate([sums_q[:K], sums_r[:K], sums_q[K:], sums_r[K:]], axis=1)
    for g in range(16):
        sums[g] = packed


def image_lined_kernel(wait, put, q, inverse, r, inner, lines, right):
    wait(0)
    for f in range(F):
        lines[pl.ds(f * K, K), :] = q[:, pl.ds(f * LANES, LANES)]
    wait(2)
    for f in range(F):
        lines[pl.ds((F + f) * K, K), :] = line(r, f)
    wait(1)
    lines[...] = dot(lines[...], inverse[...], ((1,), (1,)))
    for f in range(F):
        columns = pl.ds(f * LANES, LANES)
        right[pl.ds(0, K), columns] = lines[pl.ds(f * K, K), :]
        right[pl.ds(K, K), columns] = lines[pl.ds((F + f) * K, K), :]
    inner[...] = dot(q[...], right[...], ((1,), (1,)))


def mid_kernel(wait, put, factor, gathered, out):
    total = jnp.sum(gathered[...], axis=0)
    rhs = jnp.concatenate([gathered[g][:, 64:] for g in range(16)], axis=0)
    mid = dot(rhs.T, factor[...].reshape(512, 512)).T
    for g in range(16):
        out[g] = jnp.concatenate([mid[g * K : (g + 1) * K], total[:, :64]], axis=1)


def packed4(a, b):
    return jnp.concatenate([a[:16], a[16:], b[:16], b[16:]], axis=1)


def alpha_kernel(wait, put, arrived, inner, alpha, lower_inverse, out):
    total = jnp.sum(arrived[...], axis=0)
    mid_q, mid_r = total[:, :32], total[:, 32:64]
    gram, proj = total[:, 64:96], total[:, 96:]
    row = lax.broadcasted_iota(jnp.int32, (K, K), 0)
    column = lax.broadcasted_iota(jnp.int32, (K, K), 1)
    eye = (row == column).astype(jnp.float32)
    work = jnp.concatenate([gram, eye], axis=1)
    below = lax.broadcasted_iota(jnp.int32, (K, 1), 0)
    scale = jnp.zeros((K, 1), jnp.float32)
    for j in range(K):
        pivot = work[j : j + 1, j : j + 1]
        factor = jnp.where(below > j, work[:, j : j + 1] / pivot, 0.0)
        scale = jnp.where(below == j, lax.rsqrt(pivot), scale)
        work = work - factor * work[j : j + 1, :]
    inverse = work[:, K:] * scale
    mix = dot(inverse, dot(inverse, proj), ((0,), (0,)))
    alpha[...] = mix
    lower_inverse[...] = inverse
    coarse_mid = mid_r - dot(mid_q, mix)
    cross = inner[:, K:] - dot(inner[:, :K], mix) + dot(mid_q, coarse_mid, ((0,), (0,)))
    packed = packed4(coarse_mid, cross)
    for g in range(16):
        out[g] = packed


def sol_kernel(wait, put, factor, gathered, out):
    cross = jnp.sum(gathered[...], axis=0)[:, 64:]
    mid = jnp.concatenate([gathered[g][:, h : h + K] for g in range(16) for h in (0, K)], axis=0)
    sol = dot(factor[...].reshape(512, 512), mid)
    for g in range(16):
        at = g * K
        out[g] = jnp.concatenate([sol[at : at + 16], sol[at + 16 : at + K], cross], axis=1)


def update_kernel(wait, put, q, r, inverse, s, p, alpha, new_s, new_r, local):
    mix = alpha[...]
    wait(0)
    wait(1)
    narrow(wide(r) - dot(mix, q[...], ((0,), (0,))), new_r)
    put(1)
    wait(2)
    local[...] = dot(new_r[...], inverse[...], ((1,), (1,)))
    put(2)
    wait(3)
    wait(4)
    narrow(wide(s) + dot(mix, wide(p), ((0,), (0,))), new_s)
    put(0)


def direction_kernel(wait, put, p, basis, local, arrived, lower_inverse, new_p, left):
    total = jnp.sum(arrived[...], axis=0)
    sol = jnp.concatenate([total[:, :32], total[:, 32:64]], axis=0)
    cross = jnp.concatenate([total[:, 64:96], total[:, 96:]], axis=0)
    inverse = lower_inverse[...]
    beta = -dot(inverse, dot(inverse, cross), ((0,), (0,)))
    mix = jnp.concatenate([beta, sol], axis=0)
    wait(0)
    wait(1)
    for f in range(F):
        columns = pl.ds(f * LANES, LANES)
        left[pl.ds(0, K), columns] = line(p, f)
        left[pl.ds(K, K), columns] = line(basis, f)
    change = dot(mix, left[...], ((0,), (0,)))
    wait(2)
    narrow(wide(local) + change, new_p)
    put(0)


def swapped(array, axes):
    return lax.all_to_all(array, axes, 0, 0, tiled=True)


def on_device(solution, residual, direction, mass, coarse_basis, line_inverse, coarse_factor):
    shape = direction.shape
    s, r, p, basis = (a.reshape(-1, LANES) for a in (solution, residual, direction, coarse_basis))
    inverse = line_inverse[0, 0]
    rows, length = p.shape
    flat = (K, F * LANES)

    slabs = call(slab_kernel, [(rows // 2, LANES)] * 4, 1, 4, name="halo_slabs")(p)
    low_x, high_x, low_y, high_y = slabs
    up_sub = [(i, i + 1) for i in range(63)]
    up_inner = [(i, i + 1) for i in range(3)]
    below_y = lax.ppermute(high_y, "x", up_inner)
    above_y = lax.ppermute(low_y, "x", [(b, a) for a, b in up_inner])
    below_x = lax.ppermute(high_x, SUB, up_sub)
    above_x = lax.ppermute(low_x, SUB, [(b, a) for a, b in up_sub])

    blocks = jnp.swapaxes(coarse_factor.reshape(32, 16, 512), 0, 1)
    factor = swapped(blocks, ROWS)
    double = (2 * K, F * LANES)
    (sums_r,) = call(residual_sums_kernel, [(2 * K, K)], 3, 0, [double], 25_000_000, name="residual_sums")(p, basis, r)
    q, sums = call(image_kernel, [flat, (16, K, LANES)], 3, 1, [double], 25_000_000, unread=1, held=4, name="image")(
        p, basis, mass.reshape(16, LANES), below_x, above_x, below_y, above_y, sums_r, factor
    )
    gathered = swapped(sums, ROWS)
    (inner,) = call(image_lined_kernel, [(K, 2 * K)], 3, 0, [(2 * rows, LANES), double], 125_000_000, name="lined_image")(
        q, inverse, r
    )
    (parts,) = call(mid_kernel, [(16, K, LANES)], 0, 0, held=1, name="coarse_mid")(factor, gathered)
    arrived = swapped(parts, COLS)
    alpha, lower_inverse, spread = call(alpha_kernel, [(K, K), (K, K), (16, 16, LANES)], 0, 0, name="alpha")(
        arrived, inner
    )
    mids = swapped(spread, COLS)
    new_s, new_r, local = call(update_kernel, [(rows, LANES)] * 3, 5, 3, flops=75_000_000, name="updates")(
        q, r, inverse, s, p, alpha
    )
    (sols,) = call(sol_kernel, [(16, 16, LANES)], 0, 0, held=1, name="coarse_sol")(factor, mids)
    last = swapped(sols, ROWS)
    (new_p,) = call(direction_kernel, [(rows, LANES)], 3, 1, [double], 25_000_000, name="new_direction")(
        p, basis, local, last, lower_inverse
    )
    return new_s.reshape(shape), new_r.reshape(shape), new_p.reshape(shape)


def solution(mesh):
    torus = Mesh(mesh.devices.reshape(8, 4, 2, 4), ("z", "y", "core", "x"))
    field = P(None, None, SUB, "x", None)
    return jax.shard_map(
        on_device,
        mesh=torus,
        in_specs=(field, field, field, P(SUB, "x", None), field, P(SUB, "x", None, None), P(SUB + ("x",), None)),
        out_specs=(field, field, field),
        check_vma=False,
    )
```

```python
import jax
import jax.numpy as jnp
from jax import lax
from jax.experimental import pallas as pl
from jax.experimental.pallas import tpu as pltpu
from jax.sharding import Mesh
from jax.sharding import PartitionSpec as P

SUB = ("z", "y", "core")
ROWS = ("y", "x")
COLS = ("z", "core")
exact = lax.Precision.HIGHEST

K = 32
F = 48
LANES = 128


def dot(a, b, dims=((1,), (0,))):
    return lax.dot_general(a, b, (dims, ((), ())), precision=exact, preferred_element_type=jnp.float32)


def halves(a):
    high = a.astype(jnp.bfloat16)
    return high, (a - high.astype(jnp.float32)).astype(jnp.bfloat16)


def dot3(a, b, dims=((1,), (0,))):
    a_high, a_low = halves(a)
    b_high, b_low = halves(b)

    def part(u, v):
        return lax.dot_general(u, v, (dims, ((), ())), preferred_element_type=jnp.float32)

    return part(a_high, b_high) + (part(a_high, b_low) + part(a_low, b_high))


def line(ref, f):
    return ref[pl.ds(f, K, stride=F), :]


def place(c, x, y):
    return (c * 4 + x) * 4 + y


def wide(ref):
    return jnp.concatenate([line(ref, f) for f in range(F)], axis=1)


def narrow(value, ref):
    for f in range(F):
        ref[pl.ds(f, K, stride=F), :] = value[:, f * LANES : (f + 1) * LANES]


def call(kernel, outs, fetched, stored, scratch=(), flops=10_000_000, unread=0, name=None, held=0):
    def run(*args):
        n, m = len(args), len(outs)
        whole = n - unread - fetched
        vmem, hbm = pl.BlockSpec(memory_space=pltpu.VMEM), pl.BlockSpec(memory_space=pltpu.HBM)

        def body(*refs):
            given, made, own = refs[:n], refs[n : n + m], refs[n + m :]
            buffers, semaphores = own[: fetched + stored], own[fetched + stored : 2 * (fetched + stored)]
            rest = own[2 * (fetched + stored) :]
            fetches = [
                pltpu.make_async_copy(*three) for three in zip(given[:fetched], buffers[:fetched], semaphores[:fetched])
            ]
            stores = [
                pltpu.make_async_copy(*three) for three in zip(buffers[fetched:], made[:stored], semaphores[fetched:])
            ]
            for fetch in fetches:
                fetch.start()
            kernel(
                lambda i: fetches[i].wait(),
                lambda i: stores[i].start(),
                *buffers[:fetched],
                *given[fetched : fetched + whole],
                *buffers[fetched:],
                *made[stored:],
                *rest,
            )
            for store in stores:
                store.wait()

        sizes = [a.size for a in args[: fetched + whole]]
        for o in outs:
            sizes.append(1)
            for length in o:
                sizes[-1] *= length
        return pl.pallas_call(
            body,
            out_shape=[pltpu.HBM(o, jnp.float32) for o in outs[:stored]]
            + [jax.ShapeDtypeStruct(o, jnp.float32) for o in outs[stored:]],
            in_specs=[hbm] * fetched + [vmem] * whole + [hbm] * unread,
            out_specs=[hbm] * stored + [vmem] * (m - stored),
            scratch_shapes=[pltpu.VMEM(a.shape, jnp.float32) for a in args[:fetched]]
            + [pltpu.VMEM(o, jnp.float32) for o in outs[:stored]]
            + [pltpu.SemaphoreType.DMA] * (fetched + stored)
            + [pltpu.VMEM(shape, jnp.float32) for shape in scratch],
            compiler_params=pltpu.CompilerParams(vmem_limit_bytes=24 * 1024 * 1024),
            cost_estimate=pl.CostEstimate(flops=flops, bytes_accessed=4 * sum(sizes), transcendentals=0),
            name=name,
            )(
            *(pltpu.with_memory_space_constraint(a, pltpu.HBM) for a in args[:fetched]),
            *(pltpu.with_memory_space_constraint(a, pltpu.VMEM) for a in args[fetched : fetched + held]),
            *args[fetched + held :],
        )

    return run


def slab_kernel(p_hbm, factor, low_x, high_x, low_y, high_y, blocks, p, whole, fetched, sent):
    fetch = pltpu.make_async_copy(p_hbm, p, fetched.at[0])
    fetch.start()
    other = pltpu.make_async_copy(factor, whole, fetched.at[1])
    other.start()
    cuts = [
        pltpu.make_async_copy(whole.at[:, pl.ds(g * 512, 512)], blocks.at[g], sent.at[g]) for g in range(16)
    ]
    fetch.wait()
    other.wait()
    for cut in cuts:
        cut.start()
    at = 0
    for c in range(3):
        for x in range(2):
            for y in range(4):
                low_x[pl.ds(at * K, K), :] = line(p, place(c, x, y))
                high_x[pl.ds(at * K, K), :] = line(p, place(c, x + 2, y))
                at += 1
    at = 0
    for c in range(3):
        for x in range(4):
            for y in range(2):
                low_y[pl.ds(at * K, K), :] = line(p, place(c, x, y))
                high_y[pl.ds(at * K, K), :] = line(p, place(c, x, y + 2))
                at += 1
    for cut in cuts:
        cut.wait()


def halo_slabs(p, factor):
    rows = p.shape[0]
    hbm, vmem = pl.BlockSpec(memory_space=pltpu.HBM), pl.BlockSpec(memory_space=pltpu.VMEM)
    return pl.pallas_call(
        slab_kernel,
        out_shape=[jax.ShapeDtypeStruct((rows // 2, LANES), jnp.float32)] * 4 + [pltpu.HBM((16, K, 512), jnp.float32)],
        in_specs=[hbm] * 2,
        out_specs=[vmem] * 4 + [hbm],
        scratch_shapes=[
            pltpu.VMEM(p.shape, jnp.float32),
            pltpu.VMEM(factor.shape, jnp.float32),
            pltpu.SemaphoreType.DMA((2,)),
            pltpu.SemaphoreType.DMA((16,)),
        ],
        compiler_params=pltpu.CompilerParams(vmem_limit_bytes=24 * 1024 * 1024),
        cost_estimate=pl.CostEstimate(flops=1_000_000, bytes_accessed=5_000_000, transcendentals=0),
        name="halo_slabs",
    )(*(pltpu.with_memory_space_constraint(a, pltpu.HBM) for a in (p, factor)))


def image_kernel(wait, put, p, mass, inverse, basis, r, below_y, above_y, below_x, above_x, q, sums, inner, left, right, lines):
    lane = lax.broadcasted_iota(jnp.int32, (K, LANES), 1)

    def at(c, x, y):
        if x < 0:
            return below_x[pl.ds(((c * 2 + x + 2) * 4 + y) * K, K), :]
        if x > 3:
            return above_x[pl.ds(((c * 2 + x - 4) * 4 + y) * K, K), :]
        if y < 0:
            return below_y[pl.ds(((c * 4 + x) * 2 + y + 2) * K, K), :]
        if y > 3:
            return above_y[pl.ds(((c * 4 + x) * 2 + y - 4) * K, K), :]
        return left[pl.ds(0, K), pl.ds(place(c, x, y) * LANES, LANES)]

    wait(0)
    for f in range(F):
        left[pl.ds(0, K), pl.ds(f * LANES, LANES)] = line(p, f)
    wait(1)
    for c in range(3):
        for x in range(4):
            for y in range(4):
                f = place(c, x, y)
                center = at(c, x, y)
                near = at(c, x - 1, y) + at(c, x + 1, y) + at(c, x, y - 1) + at(c, x, y + 1)
                far = at(c, x - 2, y) + at(c, x + 2, y) + at(c, x, y - 2) + at(c, x, y + 2)
                near = near + jnp.where(lane >= 1, pltpu.roll(center, 1, 1), 0.0)
                near = near + jnp.where(lane < LANES - 1, pltpu.roll(center, LANES - 1, 1), 0.0)
                far = far + jnp.where(lane >= 2, pltpu.roll(center, 2, 1), 0.0)
                far = far + jnp.where(lane < LANES - 2, pltpu.roll(center, LANES - 2, 1), 0.0)
                weight = mass[pl.ds(x * 4 + y, 1), :] + 7.5
                value = weight * center - (4.0 / 3.0) * near + (1.0 / 12.0) * far
                q[:, pl.ds(f * LANES, LANES)] = value
                right[pl.ds(0, K), pl.ds(f * LANES, LANES)] = value
                lines[pl.ds(f * K, K), :] = value
    put(0)
    wait(2)
    lines[...] = dot3(lines[...], inverse[...])
    wait(3)
    wait(4)
    for f in range(F):
        columns = pl.ds(f * LANES, LANES)
        left[pl.ds(K, K), columns] = line(basis, f)
        left[pl.ds(2 * K, K), columns] = lines[pl.ds(f * K, K), :]
        right[pl.ds(K, K), columns] = line(r, f)
    every = dot3(left[...], right[...], ((1,), (1,)))
    sums[...] = jnp.concatenate([every[:K], every[K : 2 * K]], axis=1)
    inner[...] = every[2 * K :]


def slots(axis):
    own = lax.axis_index(axis)
    return [lax.rem(own + 4 - d, 4) for d in range(4)]


def gather_y_kernel(wait, put, sums_0, sums_1, sums_2, sums_3, out, lines):
    total = jnp.zeros((K, 64), jnp.float32)
    for slot, arrived in zip(slots("y"), (sums_0, sums_1, sums_2, sums_3)):
        lines[pl.ds(pl.multiple_of(slot * K, K), K), :] = arrived[...]
        total = total + arrived[:, :64]
    out[pl.ds(0, 64), :] = jnp.concatenate([lines[pl.ds(0, 64), :][:, 64:], lines[pl.ds(64, 64), :][:, 64:]], axis=1)
    out[pl.ds(64, 16), :] = jnp.concatenate([total[:16], total[16:]], axis=1)


def mid_kernel(wait, put, factor, group_0, group_1, group_2, group_3, out, rhs):
    total = jnp.zeros((16, LANES), jnp.float32)
    for slot, arrived in zip(slots("x"), (group_0, group_1, group_2, group_3)):
        for y in range(4):
            piece = arrived[pl.ds((y % 2) * K, K), :][:, (y // 2) * 64 : (y // 2 + 1) * 64]
            rhs[pl.ds(pl.multiple_of((y * 4 + slot) * K, K), K), :] = piece
        total = total + arrived[pl.ds(64, 16), :]
    total = jnp.concatenate([total[:, :64], total[:, 64:]], axis=0)
    mid = dot3(rhs[...].T, factor[...].reshape(512, 512)).T
    for g in range(16):
        out[g] = jnp.concatenate([mid[g * K : (g + 1) * K], total], axis=1)


def packed4(a, b):
    return jnp.concatenate([a[:16], a[16:], b[:16], b[16:]], axis=1)


def alpha_kernel(wait, put, arrived, inner, alpha, gram_inverse, out):
    total = jnp.sum(arrived[...], axis=0)
    mid_q, mid_r = total[:, :32], total[:, 32:64]
    gram, proj = total[:, 64:96], total[:, 96:]
    row = lax.broadcasted_iota(jnp.int32, (K, K), 0)
    column = lax.broadcasted_iota(jnp.int32, (K, K), 1)
    work = jnp.concatenate([gram, (row == column).astype(jnp.float32), proj], axis=1)
    at = lax.broadcasted_iota(jnp.int32, (K, 1), 0)
    for j in range(0, K, 2):
        first, second = work[j : j + 1, :], work[j + 1 : j + 2, :]
        pivot = 1.0 / first[:, j : j + 1]
        scaled = first * pivot
        second = second - second[:, j : j + 1] * scaled
        second = second * (1.0 / second[:, j + 1 : j + 2])
        first = scaled - scaled[:, j + 1 : j + 2] * second
        rest = work - work[:, j : j + 1] * first - work[:, j + 1 : j + 2] * second
        work = jnp.where(at == j, first, jnp.where(at == j + 1, second, rest))
    mix = work[:, 2 * K :]
    inverse = work[:, K : 2 * K]
    alpha[...] = mix
    gram_inverse[...] = inverse
    coarse_mid = mid_r - dot(mid_q, mix)
    cross = inner[:, K:] - dot(inner[:, :K], mix) + dot(mid_q, coarse_mid, ((0,), (0,)))
    packed = packed4(coarse_mid, cross)
    for g in range(16):
        out[g] = packed


def sol_kernel(wait, put, factor, gathered, out):
    cross = jnp.sum(gathered[...], axis=0)[:, 64:]
    mid = jnp.concatenate([gathered[g][:, h : h + K] for g in range(16) for h in (0, K)], axis=0)
    sol = dot3(factor[...].reshape(512, 512), mid)
    for g in range(16):
        at = g * K
        out[g] = jnp.concatenate([sol[at : at + 16], sol[at + 16 : at + K], cross], axis=1)


def update_kernel(wait, put, q, r, inverse, s, p, basis, alpha, new_s, new_r, local, left, lines):
    mix = alpha[...]
    wait(0)
    wait(1)
    narrow(wide(r) - dot3(mix, q[...], ((0,), (0,))), new_r)
    put(1)
    wait(2)
    lines[...] = dot3(new_r[...], inverse[...], ((1,), (1,)))
    local[...] = wide(lines)
    wait(3)
    wait(4)
    wait(5)
    for f in range(F):
        columns = pl.ds(f * LANES, LANES)
        left[pl.ds(0, K), columns] = line(p, f)
        left[pl.ds(K, K), columns] = line(basis, f)
    narrow(wide(s) + dot3(mix, left[pl.ds(0, K), :], ((0,), (0,))), new_s)
    put(0)


def direction_kernel(wait, put, left, local, arrived, gram_inverse, new_p):
    total = jnp.sum(arrived[...], axis=0)
    sol = jnp.concatenate([total[:, :32], total[:, 32:64]], axis=0)
    cross = jnp.concatenate([total[:, 64:96], total[:, 96:]], axis=0)
    beta = -dot(gram_inverse[...], cross)
    mix = jnp.concatenate([beta, sol], axis=0)
    narrow(local[...] + dot3(mix, left[...], ((0,), (0,))), new_p)
    put(0)


def swapped(array, axes):
    return lax.all_to_all(array, axes, 0, 0, tiled=True)


def from_all(array, axis):
    n = lax.axis_size(axis)
    return [array] + [lax.ppermute(array, axis, [(i, (i + d) % n) for i in range(n)]) for d in range(1, n)]


def on_device(solution, residual, direction, mass, coarse_basis, line_inverse, coarse_factor):
    shape = direction.shape
    s, r, p, basis = (a.reshape(-1, LANES) for a in (solution, residual, direction, coarse_basis))
    inverse = line_inverse[0, 0]
    rows, length = p.shape
    flat = (K, F * LANES)

    double = (2 * K, F * LANES)
    low_x, high_x, low_y, high_y, blocks = halo_slabs(p, coarse_factor)
    up_sub = [(i, i + 1) for i in range(63)]
    up_inner = [(i, i + 1) for i in range(3)]
    below_y = lax.ppermute(high_y, "x", up_inner)
    above_y = lax.ppermute(low_y, "x", [(b, a) for a, b in up_inner])
    below_x = lax.ppermute(high_x, SUB, up_sub)
    above_x = lax.ppermute(low_x, SUB, [(b, a) for a, b in up_sub])

    factor = swapped(blocks, ROWS)
    q, sums, inner = call(
        image_kernel,
        [flat, (K, LANES), (K, 2 * K)],
        5,
        1,
        [(3 * K, F * LANES), double, (rows, LANES)],
        50_000_000_000,
        held=4,
        name="image",
    )(p, mass.reshape(16, LANES), inverse, basis, r, below_y, above_y, below_x, above_x)
    (group,) = call(gather_y_kernel, [(80, LANES)], 0, 0, [(4 * K, LANES)], name="gather_y")(*from_all(sums, "y"))
    (parts,) = call(mid_kernel, [(16, K, LANES)], 0, 0, [(512, 64)], held=1, name="coarse_mid")(
        factor, *from_all(group, "x")
    )
    arrived = swapped(parts, COLS)
    alpha, gram_inverse, spread = call(alpha_kernel, [(K, K), (K, K), (16, 16, LANES)], 0, 0, name="alpha")(
        arrived, inner
    )
    mids = swapped(spread, COLS)
    new_s, new_r, local, both = call(
        update_kernel, [(rows, LANES)] * 2 + [flat, double], 6, 2, [(rows, LANES)], 75_000_000, name="updates"
    )(q, r, inverse, s, p, basis, alpha)
    (sols,) = call(sol_kernel, [(16, 16, LANES)], 0, 0, held=1, name="coarse_sol")(factor, mids)
    last = swapped(sols, ROWS)
    (new_p,) = call(direction_kernel, [(rows, LANES)], 0, 1, flops=25_000_000, held=2, name="new_direction")(
        both, local, last, gram_inverse
    )
    return new_s.reshape(shape), new_r.reshape(shape), new_p.reshape(shape)


def solution(mesh):
    torus = Mesh(mesh.devices.reshape(8, 4, 2, 4), ("z", "y", "core", "x"))
    field = P(None, None, SUB, "x", None)
    return jax.shard_map(
        on_device,
        mesh=torus,
        in_specs=(field, field, field, P(SUB, "x", None), field, P(SUB, "x", None, None), P(SUB + ("x",), None)),
        out_specs=(field, field, field),
        check_vma=False,
    )
```

```python
import jax
import jax.numpy as jnp
from jax import lax
from jax.experimental import pallas as pl
from jax.experimental.pallas import tpu as pltpu
from jax.sharding import Mesh
from jax.sharding import PartitionSpec as P

SUB = ("z", "y", "core")
ROWS = ("y", "x")
COLS = ("core", "z")
exact = lax.Precision.HIGHEST

K = 32
F = 48
LANES = 128


def dot(a, b, dims=((1,), (0,))):
    return lax.dot_general(a, b, (dims, ((), ())), precision=exact, preferred_element_type=jnp.float32)


def halves(a):
    high = a.astype(jnp.bfloat16)
    return high, (a - high.astype(jnp.float32)).astype(jnp.bfloat16)


def dot3(a, b, dims=((1,), (0,))):
    a_high, a_low = halves(a)
    b_high, b_low = halves(b)

    def part(u, v):
        return lax.dot_general(u, v, (dims, ((), ())), preferred_element_type=jnp.float32)

    return part(a_high, b_high) + (part(a_high, b_low) + part(a_low, b_high))


def line(ref, f):
    return ref[pl.ds(f, K, stride=F), :]


def place(c, x, y):
    return (c * 4 + x) * 4 + y


def wide(ref):
    return jnp.concatenate([line(ref, f) for f in range(F)], axis=1)


def narrow(value, ref):
    for f in range(F):
        ref[pl.ds(f, K, stride=F), :] = value[:, f * LANES : (f + 1) * LANES]


def call(kernel, outs, fetched, stored, scratch=(), flops=10_000_000, unread=0, name=None, held=0):
    def run(*args):
        n, m = len(args), len(outs)
        whole = n - unread - fetched
        vmem, hbm = pl.BlockSpec(memory_space=pltpu.VMEM), pl.BlockSpec(memory_space=pltpu.HBM)

        def body(*refs):
            given, made, own = refs[:n], refs[n : n + m], refs[n + m :]
            buffers, semaphores = own[: fetched + stored], own[fetched + stored : 2 * (fetched + stored)]
            rest = own[2 * (fetched + stored) :]
            fetches = [
                pltpu.make_async_copy(*three) for three in zip(given[:fetched], buffers[:fetched], semaphores[:fetched])
            ]
            stores = [
                pltpu.make_async_copy(*three) for three in zip(buffers[fetched:], made[:stored], semaphores[fetched:])
            ]
            for fetch in fetches:
                fetch.start()
            kernel(
                lambda i: fetches[i].wait(),
                lambda i: stores[i].start(),
                *buffers[:fetched],
                *given[fetched : fetched + whole],
                *buffers[fetched:],
                *made[stored:],
                *rest,
            )
            for store in stores:
                store.wait()

        sizes = [a.size for a in args[: fetched + whole]]
        for o in outs:
            sizes.append(1)
            for length in o:
                sizes[-1] *= length
        return pl.pallas_call(
            body,
            out_shape=[pltpu.HBM(o, jnp.float32) for o in outs[:stored]]
            + [jax.ShapeDtypeStruct(o, jnp.float32) for o in outs[stored:]],
            in_specs=[hbm] * fetched + [vmem] * whole + [hbm] * unread,
            out_specs=[hbm] * stored + [vmem] * (m - stored),
            scratch_shapes=[pltpu.VMEM(a.shape, jnp.float32) for a in args[:fetched]]
            + [pltpu.VMEM(o, jnp.float32) for o in outs[:stored]]
            + [pltpu.SemaphoreType.DMA] * (fetched + stored)
            + [pltpu.VMEM(shape, jnp.float32) for shape in scratch],
            compiler_params=pltpu.CompilerParams(vmem_limit_bytes=24 * 1024 * 1024),
            cost_estimate=pl.CostEstimate(flops=flops, bytes_accessed=4 * sum(sizes), transcendentals=0),
            name=name,
            )(
            *(pltpu.with_memory_space_constraint(a, pltpu.HBM) for a in args[:fetched]),
            *(pltpu.with_memory_space_constraint(a, pltpu.VMEM) for a in args[fetched : fetched + held]),
            *args[fetched + held :],
        )

    return run


def slab_kernel(p_hbm, factor, low_x, high_x, low_y, high_y, blocks, p, whole, fetched, sent):
    fetch = pltpu.make_async_copy(p_hbm, p, fetched.at[0])
    fetch.start()
    other = pltpu.make_async_copy(factor, whole, fetched.at[1])
    other.start()
    cuts = [
        pltpu.make_async_copy(whole.at[:, pl.ds(g * 512, 512)], blocks.at[g], sent.at[g]) for g in range(16)
    ]
    fetch.wait()
    other.wait()
    for cut in cuts:
        cut.start()
    at = 0
    for c in range(3):
        for x in range(2):
            for y in range(4):
                low_x[pl.ds(at * K, K), :] = line(p, place(c, x, y))
                high_x[pl.ds(at * K, K), :] = line(p, place(c, x + 2, y))
                at += 1
    at = 0
    for c in range(3):
        for x in range(4):
            for y in range(2):
                low_y[pl.ds(at * K, K), :] = line(p, place(c, x, y))
                high_y[pl.ds(at * K, K), :] = line(p, place(c, x, y + 2))
                at += 1
    for cut in cuts:
        cut.wait()


def halo_slabs(p, factor):
    rows = p.shape[0]
    hbm, vmem = pl.BlockSpec(memory_space=pltpu.HBM), pl.BlockSpec(memory_space=pltpu.VMEM)
    return pl.pallas_call(
        slab_kernel,
        out_shape=[jax.ShapeDtypeStruct((rows // 2, LANES), jnp.float32)] * 4 + [pltpu.HBM((16, K, 512), jnp.float32)],
        in_specs=[hbm] * 2,
        out_specs=[vmem] * 4 + [hbm],
        scratch_shapes=[
            pltpu.VMEM(p.shape, jnp.float32),
            pltpu.VMEM(factor.shape, jnp.float32),
            pltpu.SemaphoreType.DMA((2,)),
            pltpu.SemaphoreType.DMA((16,)),
        ],
        compiler_params=pltpu.CompilerParams(vmem_limit_bytes=24 * 1024 * 1024),
        cost_estimate=pl.CostEstimate(flops=1_000_000, bytes_accessed=5_000_000, transcendentals=0),
        name="halo_slabs",
    )(*(pltpu.with_memory_space_constraint(a, pltpu.HBM) for a in (p, factor)))


def image_kernel(wait, put, p, mass, inverse, basis, r, below_x, below_y, above_y, above_x, q, sums, inner, left, right, lines):
    lane = lax.broadcasted_iota(jnp.int32, (K, LANES), 1)

    def at(c, x, y):
        if x < 0:
            return below_x[pl.ds(((c * 2 + x + 2) * 4 + y) * K, K), :]
        if x > 3:
            return above_x[pl.ds(((c * 2 + x - 4) * 4 + y) * K, K), :]
        if y < 0:
            return below_y[pl.ds(((c * 4 + x) * 2 + y + 2) * K, K), :]
        if y > 3:
            return above_y[pl.ds(((c * 4 + x) * 2 + y - 4) * K, K), :]
        return left[pl.ds(0, K), pl.ds(place(c, x, y) * LANES, LANES)]

    wait(0)
    for f in range(F):
        left[pl.ds(0, K), pl.ds(f * LANES, LANES)] = line(p, f)
    wait(1)
    for c in range(3):
        for x in range(4):
            for y in range(4):
                f = place(c, x, y)
                center = at(c, x, y)
                near = at(c, x - 1, y) + at(c, x + 1, y) + at(c, x, y - 1) + at(c, x, y + 1)
                far = at(c, x - 2, y) + at(c, x + 2, y) + at(c, x, y - 2) + at(c, x, y + 2)
                near = near + jnp.where(lane >= 1, pltpu.roll(center, 1, 1), 0.0)
                near = near + jnp.where(lane < LANES - 1, pltpu.roll(center, LANES - 1, 1), 0.0)
                far = far + jnp.where(lane >= 2, pltpu.roll(center, 2, 1), 0.0)
                far = far + jnp.where(lane < LANES - 2, pltpu.roll(center, LANES - 2, 1), 0.0)
                weight = mass[pl.ds(x * 4 + y, 1), :] + 7.5
                value = weight * center - (4.0 / 3.0) * near + (1.0 / 12.0) * far
                q[:, pl.ds(f * LANES, LANES)] = value
                right[pl.ds(0, K), pl.ds(f * LANES, LANES)] = value
                lines[pl.ds(f * K, K), :] = value
    put(0)
    wait(2)
    lines[...] = dot3(lines[...], inverse[...])
    wait(3)
    wait(4)
    for f in range(F):
        columns = pl.ds(f * LANES, LANES)
        left[pl.ds(K, K), columns] = line(basis, f)
        left[pl.ds(2 * K, K), columns] = lines[pl.ds(f * K, K), :]
        right[pl.ds(K, K), columns] = line(r, f)
    every = dot3(left[...], right[...], ((1,), (1,)))
    sums[...] = jnp.concatenate([every[:K], every[K : 2 * K]], axis=1)
    inner[...] = every[2 * K :]


def slots(axis):
    own = lax.axis_index(axis)
    return [lax.rem(own + 4 - d, 4) for d in range(4)]


def gather_y_kernel(wait, put, sums_0, sums_1, sums_2, sums_3, out, lines):
    total = jnp.zeros((K, 64), jnp.float32)
    for slot, arrived in zip(slots("y"), (sums_0, sums_1, sums_2, sums_3)):
        lines[pl.ds(pl.multiple_of(slot * K, K), K), :] = arrived[...]
        total = total + arrived[:, :64]
    out[pl.ds(0, 64), :] = jnp.concatenate([lines[pl.ds(0, 64), :][:, 64:], lines[pl.ds(64, 64), :][:, 64:]], axis=1)
    out[pl.ds(64, 16), :] = jnp.concatenate([total[:16], total[16:]], axis=1)


def mid_kernel(wait, put, factor, group_0, group_1, group_2, group_3, out, rhs):
    total = jnp.zeros((16, LANES), jnp.float32)
    for slot, arrived in zip(slots("x"), (group_0, group_1, group_2, group_3)):
        for y in range(4):
            piece = arrived[pl.ds((y % 2) * K, K), :][:, (y // 2) * 64 : (y // 2 + 1) * 64]
            rhs[pl.ds(pl.multiple_of((y * 4 + slot) * K, K), K), :] = piece
        total = total + arrived[pl.ds(64, 16), :]
    total = jnp.concatenate([total[:, :64], total[:, 64:]], axis=0)
    mid = dot3(rhs[...].T, factor[...].reshape(512, 512)).T
    for g in range(16):
        out[g] = jnp.concatenate([mid[g * K : (g + 1) * K], total], axis=1)


def packed4(a, b):
    return jnp.concatenate([a[:16], a[16:], b[:16], b[16:]], axis=1)


def alpha_kernel(wait, put, arrived, inner, alpha, gram_inverse, out):
    total = jnp.sum(arrived[...], axis=0)
    mid_q, mid_r = total[:, :32], total[:, 32:64]
    gram, proj = total[:, 64:96], total[:, 96:]
    base = inner[...] + dot(mid_q, total[:, : 2 * K], ((0,), (0,)))
    row = lax.broadcasted_iota(jnp.int32, (K, K), 0)
    column = lax.broadcasted_iota(jnp.int32, (K, K), 1)
    work = jnp.concatenate([gram, (row == column).astype(jnp.float32), proj], axis=1)
    at = lax.broadcasted_iota(jnp.int32, (K, 1), 0)
    for j in range(0, K, 2):
        first, second = work[j : j + 1, :], work[j + 1 : j + 2, :]
        pivot = 1.0 / first[:, j : j + 1]
        scaled = first * pivot
        second = second - second[:, j : j + 1] * scaled
        second = second * (1.0 / second[:, j + 1 : j + 2])
        first = scaled - scaled[:, j + 1 : j + 2] * second
        rest = work - work[:, j : j + 1] * first - work[:, j + 1 : j + 2] * second
        work = jnp.where(at == j, first, jnp.where(at == j + 1, second, rest))
    mix = work[:, 2 * K :]
    inverse = work[:, K : 2 * K]
    alpha[...] = mix
    gram_inverse[...] = inverse
    after = dot(jnp.concatenate([mid_q, base[:, :K]], axis=0), mix)
    coarse_mid = mid_r - after[:K]
    cross = base[:, K:] - after[K:]
    packed = packed4(coarse_mid, cross)
    for g in range(16):
        out[g] = packed


def sol_kernel(wait, put, factor, gathered, out):
    cross = jnp.sum(gathered[...], axis=0)[:, 64:]
    mid = jnp.concatenate([gathered[g][:, h : h + K] for g in range(16) for h in (0, K)], axis=0)
    sol = dot3(factor[...].reshape(512, 512), mid)
    for g in range(16):
        at = g * K
        out[g] = jnp.concatenate([sol[at : at + 16], sol[at + 16 : at + K], cross], axis=1)


def update_kernel(wait, put, q, r, inverse, s, p, basis, alpha, new_s, new_r, local, left, lines):
    mix = alpha[...]
    wait(0)
    wait(1)
    narrow(wide(r) - dot3(mix, q[...], ((0,), (0,))), new_r)
    put(1)
    wait(2)
    lines[...] = dot3(new_r[...], inverse[...], ((1,), (1,)))
    local[...] = wide(lines)
    wait(3)
    wait(4)
    wait(5)
    for f in range(F):
        columns = pl.ds(f * LANES, LANES)
        left[pl.ds(0, K), columns] = line(p, f)
        left[pl.ds(K, K), columns] = line(basis, f)
    narrow(wide(s) + dot3(mix, left[pl.ds(0, K), :], ((0,), (0,))), new_s)
    put(0)


def direction_kernel(wait, put, left, local, arrived, gram_inverse, new_p):
    total = jnp.sum(arrived[...], axis=0)
    sol = jnp.concatenate([total[:, :32], total[:, 32:64]], axis=0)
    cross = jnp.concatenate([total[:, 64:96], total[:, 96:]], axis=0)
    beta = -dot(gram_inverse[...], cross)
    mix = jnp.concatenate([beta, sol], axis=0)
    narrow(local[...] + dot3(mix, left[...], ((0,), (0,))), new_p)
    put(0)


def swapped(array, axes):
    return lax.all_to_all(array, axes, 0, 0, tiled=True)


def from_all(array, axis):
    n = lax.axis_size(axis)
    return [array] + [lax.ppermute(array, axis, [(i, (i + d) % n) for i in range(n)]) for d in range(1, n)]


def on_device(solution, residual, direction, mass, coarse_basis, line_inverse, coarse_factor):
    shape = direction.shape
    s, r, p, basis = (a.reshape(-1, LANES) for a in (solution, residual, direction, coarse_basis))
    inverse = line_inverse[0, 0]
    rows, length = p.shape
    flat = (K, F * LANES)

    double = (2 * K, F * LANES)
    low_x, high_x, low_y, high_y, blocks = halo_slabs(p, coarse_factor)
    up_sub = [(i, i + 1) for i in range(63)]
    up_inner = [(i, i + 1) for i in range(3)]
    below_x = lax.ppermute(high_x, SUB, up_sub)
    above_x = lax.ppermute(low_x, SUB, [(b, a) for a, b in up_sub])

    below_y = lax.ppermute(high_y, "x", up_inner)
    above_y = lax.ppermute(low_y, "x", [(b, a) for a, b in up_inner])
    factor = swapped(blocks, ROWS)
    q, sums, inner = call(
        image_kernel,
        [flat, (K, LANES), (K, 2 * K)],
        5,
        1,
        [(3 * K, F * LANES), double, (rows, LANES)],
        50_000_000_000,
        held=4,
        name="image",
    )(p, mass.reshape(16, LANES), inverse, basis, r, below_x, below_y, above_y, above_x)
    (group,) = call(gather_y_kernel, [(80, LANES)], 0, 0, [(4 * K, LANES)], name="gather_y")(*from_all(sums, "y"))
    (parts,) = call(mid_kernel, [(16, K, LANES)], 0, 0, [(512, 64)], held=1, name="coarse_mid")(
        factor, *from_all(group, "x")
    )
    arrived = swapped(parts, COLS)
    alpha, gram_inverse, spread = call(alpha_kernel, [(K, K), (K, K), (16, 16, LANES)], 0, 0, name="alpha")(
        arrived, inner
    )
    mids = swapped(spread, COLS)
    new_s, new_r, local, both = call(
        update_kernel, [(rows, LANES)] * 2 + [flat, double], 6, 2, [(rows, LANES)], 75_000_000, name="updates"
    )(q, r, inverse, s, p, basis, alpha)
    (sols,) = call(sol_kernel, [(16, 16, LANES)], 0, 0, held=1, name="coarse_sol")(factor, mids)
    last = swapped(sols, ROWS)
    (new_p,) = call(direction_kernel, [(rows, LANES)], 0, 1, flops=25_000_000, held=2, name="new_direction")(
        both, local, last, gram_inverse
    )
    return new_s.reshape(shape), new_r.reshape(shape), new_p.reshape(shape)


def solution(mesh):
    torus = Mesh(mesh.devices.reshape(8, 4, 2, 4), ("z", "y", "core", "x"))
    field = P(None, None, SUB, "x", None)
    return jax.shard_map(
        on_device,
        mesh=torus,
        in_specs=(field, field, field, P(SUB, "x", None), field, P(SUB, "x", None, None), P(SUB + ("x",), None)),
        out_specs=(field, field, field),
        check_vma=False,
    )
```

```python
import jax
import jax.numpy as jnp
from jax import lax
from jax.experimental import pallas as pl
from jax.experimental.pallas import tpu as pltpu
from jax.sharding import Mesh
from jax.sharding import PartitionSpec as P

SUB = ("z", "y", "core")
ROWS = ("y", "x")
COLS = ("core", "z")
exact = lax.Precision.HIGHEST

K = 32
F = 48
LANES = 128


def dot(a, b, dims=((1,), (0,))):
    return lax.dot_general(a, b, (dims, ((), ())), precision=exact, preferred_element_type=jnp.float32)


def halves(a):
    high = a.astype(jnp.bfloat16)
    return high, (a - high.astype(jnp.float32)).astype(jnp.bfloat16)


def dot3(a, b, dims=((1,), (0,))):
    a_high, a_low = halves(a)
    b_high, b_low = halves(b)

    def part(u, v):
        return lax.dot_general(u, v, (dims, ((), ())), preferred_element_type=jnp.float32)

    return part(a_high, b_high) + (part(a_high, b_low) + part(a_low, b_high))


def line(ref, f):
    return ref[pl.ds(f, K, stride=F), :]


def place(c, x, y):
    return (c * 4 + x) * 4 + y


def wide(ref):
    return jnp.concatenate([line(ref, f) for f in range(F)], axis=1)


def narrow(value, ref):
    for f in range(F):
        ref[pl.ds(f, K, stride=F), :] = value[:, f * LANES : (f + 1) * LANES]


def call(kernel, outs, fetched, stored, scratch=(), flops=10_000_000, unread=0, name=None, held=0):
    def run(*args):
        n, m = len(args), len(outs)
        whole = n - unread - fetched
        vmem, hbm = pl.BlockSpec(memory_space=pltpu.VMEM), pl.BlockSpec(memory_space=pltpu.HBM)

        def body(*refs):
            given, made, own = refs[:n], refs[n : n + m], refs[n + m :]
            buffers, semaphores = own[: fetched + stored], own[fetched + stored : 2 * (fetched + stored)]
            rest = own[2 * (fetched + stored) :]
            fetches = [
                pltpu.make_async_copy(*three) for three in zip(given[:fetched], buffers[:fetched], semaphores[:fetched])
            ]
            stores = [
                pltpu.make_async_copy(*three) for three in zip(buffers[fetched:], made[:stored], semaphores[fetched:])
            ]
            for fetch in fetches:
                fetch.start()
            kernel(
                lambda i: fetches[i].wait(),
                lambda i: stores[i].start(),
                *buffers[:fetched],
                *given[fetched : fetched + whole],
                *buffers[fetched:],
                *made[stored:],
                *rest,
            )
            for store in stores:
                store.wait()

        sizes = [a.size for a in args[: fetched + whole]]
        for o in outs:
            sizes.append(1)
            for length in o:
                sizes[-1] *= length
        return pl.pallas_call(
            body,
            out_shape=[pltpu.HBM(o, jnp.float32) for o in outs[:stored]]
            + [jax.ShapeDtypeStruct(o, jnp.float32) for o in outs[stored:]],
            in_specs=[hbm] * fetched + [vmem] * whole + [hbm] * unread,
            out_specs=[hbm] * stored + [vmem] * (m - stored),
            scratch_shapes=[pltpu.VMEM(a.shape, jnp.float32) for a in args[:fetched]]
            + [pltpu.VMEM(o, jnp.float32) for o in outs[:stored]]
            + [pltpu.SemaphoreType.DMA] * (fetched + stored)
            + [pltpu.VMEM(shape, jnp.float32) for shape in scratch],
            compiler_params=pltpu.CompilerParams(vmem_limit_bytes=24 * 1024 * 1024),
            cost_estimate=pl.CostEstimate(flops=flops, bytes_accessed=4 * sum(sizes), transcendentals=0),
            name=name,
            )(
            *(pltpu.with_memory_space_constraint(a, pltpu.HBM) for a in args[:fetched]),
            *(pltpu.with_memory_space_constraint(a, pltpu.VMEM) for a in args[fetched : fetched + held]),
            *args[fetched + held :],
        )

    return run


def slab_kernel(p_hbm, factor, low_x, high_x, low_y, high_y, blocks, p, whole, fetched, sent):
    fetch = pltpu.make_async_copy(p_hbm, p, fetched.at[4])
    fetch.start()
    parts = [
        pltpu.make_async_copy(
            factor.at[:, pl.ds(i * 2048, 2048)], whole.at[:, pl.ds(i * 2048, 2048)], fetched.at[i]
        )
        for i in range(4)
    ]
    for part in parts:
        part.start()
    cuts = [
        pltpu.make_async_copy(whole.at[:, pl.ds(g * 512, 512)], blocks.at[g], sent.at[g]) for g in range(16)
    ]
    for i, part in enumerate(parts):
        part.wait()
        for cut in cuts[4 * i : 4 * i + 4]:
            cut.start()
    fetch.wait()
    at = 0
    for c in range(3):
        for x in range(2):
            for y in range(4):
                low_x[pl.ds(at * K, K), :] = line(p, place(c, x, y))
                high_x[pl.ds(at * K, K), :] = line(p, place(c, x + 2, y))
                at += 1
    at = 0
    for c in range(3):
        for x in range(4):
            for y in range(2):
                low_y[pl.ds(at * K, K), :] = line(p, place(c, x, y))
                high_y[pl.ds(at * K, K), :] = line(p, place(c, x, y + 2))
                at += 1
    for cut in cuts:
        cut.wait()


def halo_slabs(p, factor):
    rows = p.shape[0]
    hbm, vmem = pl.BlockSpec(memory_space=pltpu.HBM), pl.BlockSpec(memory_space=pltpu.VMEM)
    return pl.pallas_call(
        slab_kernel,
        out_shape=[jax.ShapeDtypeStruct((rows // 2, LANES), jnp.float32)] * 4 + [pltpu.HBM((16, K, 512), jnp.float32)],
        in_specs=[hbm] * 2,
        out_specs=[vmem] * 4 + [hbm],
        scratch_shapes=[
            pltpu.VMEM(p.shape, jnp.float32),
            pltpu.VMEM(factor.shape, jnp.float32),
            pltpu.SemaphoreType.DMA((5,)),
            pltpu.SemaphoreType.DMA((16,)),
        ],
        compiler_params=pltpu.CompilerParams(vmem_limit_bytes=24 * 1024 * 1024),
        cost_estimate=pl.CostEstimate(flops=1_000_000, bytes_accessed=5_000_000, transcendentals=0),
        name="halo_slabs",
    )(*(pltpu.with_memory_space_constraint(a, pltpu.HBM) for a in (p, factor)))


def image_kernel(wait, put, p, mass, inverse, basis, r, below_x, below_y, above_y, above_x, q, sums, inner, left, right, lines):
    lane = lax.broadcasted_iota(jnp.int32, (K, LANES), 1)

    def at(c, x, y):
        if x < 0:
            return below_x[pl.ds(((c * 2 + x + 2) * 4 + y) * K, K), :]
        if x > 3:
            return above_x[pl.ds(((c * 2 + x - 4) * 4 + y) * K, K), :]
        if y < 0:
            return below_y[pl.ds(((c * 4 + x) * 2 + y + 2) * K, K), :]
        if y > 3:
            return above_y[pl.ds(((c * 4 + x) * 2 + y - 4) * K, K), :]
        return left[pl.ds(0, K), pl.ds(place(c, x, y) * LANES, LANES)]

    wait(0)
    for f in range(F):
        left[pl.ds(0, K), pl.ds(f * LANES, LANES)] = line(p, f)
    wait(1)
    for c in range(3):
        for x in range(4):
            for y in range(4):
                f = place(c, x, y)
                center = at(c, x, y)
                near = at(c, x - 1, y) + at(c, x + 1, y) + at(c, x, y - 1) + at(c, x, y + 1)
                far = at(c, x - 2, y) + at(c, x + 2, y) + at(c, x, y - 2) + at(c, x, y + 2)
                near = near + jnp.where(lane >= 1, pltpu.roll(center, 1, 1), 0.0)
                near = near + jnp.where(lane < LANES - 1, pltpu.roll(center, LANES - 1, 1), 0.0)
                far = far + jnp.where(lane >= 2, pltpu.roll(center, 2, 1), 0.0)
                far = far + jnp.where(lane < LANES - 2, pltpu.roll(center, LANES - 2, 1), 0.0)
                weight = mass[pl.ds(x * 4 + y, 1), :] + 7.5
                value = weight * center - (4.0 / 3.0) * near + (1.0 / 12.0) * far
                q[:, pl.ds(f * LANES, LANES)] = value
                right[pl.ds(0, K), pl.ds(f * LANES, LANES)] = value
                lines[pl.ds(f * K, K), :] = value
    put(0)
    wait(2)
    lines[...] = dot3(lines[...], inverse[...])
    wait(3)
    wait(4)
    for f in range(F):
        columns = pl.ds(f * LANES, LANES)
        left[pl.ds(K, K), columns] = line(basis, f)
        left[pl.ds(2 * K, K), columns] = lines[pl.ds(f * K, K), :]
        right[pl.ds(K, K), columns] = line(r, f)
    every = dot3(left[...], right[...], ((1,), (1,)))
    sums[...] = jnp.concatenate([every[:K], every[K : 2 * K]], axis=1)
    inner[...] = every[2 * K :]


def slots(axis):
    own = lax.axis_index(axis)
    return [lax.rem(own + 4 - d, 4) for d in range(4)]


def gather_y_kernel(wait, put, sums_0, sums_1, sums_2, sums_3, out, lines):
    total = jnp.zeros((K, 64), jnp.float32)
    for slot, arrived in zip(slots("y"), (sums_0, sums_1, sums_2, sums_3)):
        lines[pl.ds(pl.multiple_of(slot * K, K), K), :] = arrived[...]
        total = total + arrived[:, :64]
    out[pl.ds(0, 64), :] = jnp.concatenate([lines[pl.ds(0, 64), :][:, 64:], lines[pl.ds(64, 64), :][:, 64:]], axis=1)
    out[pl.ds(64, 16), :] = jnp.concatenate([total[:16], total[16:]], axis=1)


def mid_kernel(wait, put, factor, group_0, group_1, group_2, group_3, out, rhs):
    total = jnp.zeros((16, LANES), jnp.float32)
    for slot, arrived in zip(slots("x"), (group_0, group_1, group_2, group_3)):
        for y in range(4):
            piece = arrived[pl.ds((y % 2) * K, K), :][:, (y // 2) * 64 : (y // 2 + 1) * 64]
            rhs[pl.ds(pl.multiple_of((y * 4 + slot) * K, K), K), :] = piece
        total = total + arrived[pl.ds(64, 16), :]
    total = jnp.concatenate([total[:, :64], total[:, 64:]], axis=0)
    mid = dot3(rhs[...].T, factor[...].reshape(512, 512)).T
    for g in range(16):
        out[g] = jnp.concatenate([mid[g * K : (g + 1) * K], total], axis=1)


def packed4(a, b):
    return jnp.concatenate([a[:16], a[16:], b[:16], b[16:]], axis=1)


def alpha_kernel(wait, put, arrived, inner, alpha, gram_inverse, out):
    total = jnp.sum(arrived[...], axis=0)
    mid_q, mid_r = total[:, :32], total[:, 32:64]
    gram, proj = total[:, 64:96], total[:, 96:]
    base = inner[...] + dot(mid_q, total[:, : 2 * K], ((0,), (0,)))
    row = lax.broadcasted_iota(jnp.int32, (K, K), 0)
    column = lax.broadcasted_iota(jnp.int32, (K, K), 1)
    work = jnp.concatenate([gram, (row == column).astype(jnp.float32), proj], axis=1)
    at = lax.broadcasted_iota(jnp.int32, (K, 1), 0)
    for j in range(0, K, 2):
        first, second = work[j : j + 1, :], work[j + 1 : j + 2, :]
        pivot = 1.0 / first[:, j : j + 1]
        scaled = first * pivot
        second = second - second[:, j : j + 1] * scaled
        second = second * (1.0 / second[:, j + 1 : j + 2])
        first = scaled - scaled[:, j + 1 : j + 2] * second
        rest = work - work[:, j : j + 1] * first - work[:, j + 1 : j + 2] * second
        work = jnp.where(at == j, first, jnp.where(at == j + 1, second, rest))
    mix = work[:, 2 * K :]
    inverse = work[:, K : 2 * K]
    alpha[...] = mix
    gram_inverse[...] = inverse
    after = dot(jnp.concatenate([mid_q, base[:, :K]], axis=0), mix)
    coarse_mid = mid_r - after[:K]
    cross = base[:, K:] - after[K:]
    packed = packed4(coarse_mid, cross)
    for g in range(16):
        out[g] = packed


def sol_kernel(wait, put, factor, gathered, out):
    cross = jnp.sum(gathered[...], axis=0)[:, 64:]
    mid = jnp.concatenate([gathered[g][:, h : h + K] for g in range(16) for h in (0, K)], axis=0)
    sol = dot3(factor[...].reshape(512, 512), mid)
    for g in range(16):
        at = g * K
        out[g] = jnp.concatenate([sol[at : at + 16], sol[at + 16 : at + K], cross], axis=1)


def update_kernel(wait, put, q, r, inverse, s, p, basis, alpha, new_s, new_r, local, left, lines):
    mix = alpha[...]
    wait(0)
    wait(1)
    narrow(wide(r) - dot3(mix, q[...], ((0,), (0,))), new_r)
    put(1)
    wait(2)
    lines[...] = dot3(new_r[...], inverse[...], ((1,), (1,)))
    local[...] = wide(lines)
    wait(3)
    wait(4)
    wait(5)
    for f in range(F):
        columns = pl.ds(f * LANES, LANES)
        left[pl.ds(0, K), columns] = line(p, f)
        left[pl.ds(K, K), columns] = line(basis, f)
    narrow(wide(s) + dot3(mix, left[pl.ds(0, K), :], ((0,), (0,))), new_s)
    put(0)


def direction_kernel(wait, put, left, local, arrived, gram_inverse, new_p):
    total = jnp.sum(arrived[...], axis=0)
    sol = jnp.concatenate([total[:, :32], total[:, 32:64]], axis=0)
    cross = jnp.concatenate([total[:, 64:96], total[:, 96:]], axis=0)
    beta = -dot(gram_inverse[...], cross)
    mix = jnp.concatenate([beta, sol], axis=0)
    narrow(local[...] + dot3(mix, left[...], ((0,), (0,))), new_p)
    put(0)


def swapped(array, axes):
    return lax.all_to_all(array, axes, 0, 0, tiled=True)


def from_all(array, axis):
    n = lax.axis_size(axis)
    return [array] + [lax.ppermute(array, axis, [(i, (i + d) % n) for i in range(n)]) for d in range(1, n)]


def on_device(solution, residual, direction, mass, coarse_basis, line_inverse, coarse_factor):
    shape = direction.shape
    s, r, p, basis = (a.reshape(-1, LANES) for a in (solution, residual, direction, coarse_basis))
    inverse = line_inverse[0, 0]
    rows, length = p.shape
    flat = (K, F * LANES)

    double = (2 * K, F * LANES)
    low_x, high_x, low_y, high_y, blocks = halo_slabs(p, coarse_factor)
    up_sub = [(i, i + 1) for i in range(63)]
    up_inner = [(i, i + 1) for i in range(3)]
    below_x = lax.ppermute(high_x, SUB, up_sub)
    above_x = lax.ppermute(low_x, SUB, [(b, a) for a, b in up_sub])

    below_y = lax.ppermute(high_y, "x", up_inner)
    above_y = lax.ppermute(low_y, "x", [(b, a) for a, b in up_inner])
    factor = swapped(blocks, ROWS)
    q, sums, inner = call(
        image_kernel,
        [flat, (K, LANES), (K, 2 * K)],
        5,
        1,
        [(3 * K, F * LANES), double, (rows, LANES)],
        50_000_000_000,
        held=4,
        name="image",
    )(p, mass.reshape(16, LANES), inverse, basis, r, below_x, below_y, above_y, above_x)
    (group,) = call(gather_y_kernel, [(80, LANES)], 0, 0, [(4 * K, LANES)], name="gather_y")(*from_all(sums, "y"))
    (parts,) = call(mid_kernel, [(16, K, LANES)], 0, 0, [(512, 64)], held=1, name="coarse_mid")(
        factor, *from_all(group, "x")
    )
    arrived = swapped(parts, COLS)
    alpha, gram_inverse, spread = call(alpha_kernel, [(K, K), (K, K), (16, 16, LANES)], 0, 0, name="alpha")(
        arrived, inner
    )
    mids = swapped(spread, COLS)
    new_s, new_r, local, both = call(
        update_kernel, [(rows, LANES)] * 2 + [flat, double], 6, 2, [(rows, LANES)], 75_000_000, name="updates"
    )(q, r, inverse, s, p, basis, alpha)
    (sols,) = call(sol_kernel, [(16, 16, LANES)], 0, 0, held=1, name="coarse_sol")(factor, mids)
    last = swapped(sols, ROWS)
    (new_p,) = call(direction_kernel, [(rows, LANES)], 0, 1, flops=25_000_000, held=2, name="new_direction")(
        both, local, last, gram_inverse
    )
    return new_s.reshape(shape), new_r.reshape(shape), new_p.reshape(shape)


def solution(mesh):
    torus = Mesh(mesh.devices.reshape(8, 4, 2, 4), ("z", "y", "core", "x"))
    field = P(None, None, SUB, "x", None)
    return jax.shard_map(
        on_device,
        mesh=torus,
        in_specs=(field, field, field, P(SUB, "x", None), field, P(SUB, "x", None, None), P(SUB + ("x",), None)),
        out_specs=(field, field, field),
        check_vma=False,
    )
```

```python
import jax
import jax.numpy as jnp
from jax import lax
from jax.experimental import pallas as pl
from jax.experimental.pallas import tpu as pltpu
from jax.sharding import Mesh
from jax.sharding import PartitionSpec as P

SUB = ("z", "y", "core")
ROWS = ("y", "x")
COLS = ("core", "z")
exact = lax.Precision.HIGHEST

K = 32
F = 48
LANES = 128


def dot(a, b, dims=((1,), (0,))):
    return lax.dot_general(a, b, (dims, ((), ())), precision=exact, preferred_element_type=jnp.float32)


def halves(a):
    high = a.astype(jnp.bfloat16)
    return high, (a - high.astype(jnp.float32)).astype(jnp.bfloat16)


def dot3(a, b, dims=((1,), (0,))):
    a_high, a_low = halves(a)
    b_high, b_low = halves(b)

    def part(u, v):
        return lax.dot_general(u, v, (dims, ((), ())), preferred_element_type=jnp.float32)

    if dims[0] == (1,) and a.shape[0] <= 512:
        both = part(jnp.concatenate([a_high, a_low], axis=0), b_high)
        return both[: a.shape[0]] + (part(a_high, b_low) + both[a.shape[0] :])
    return part(a_high, b_high) + (part(a_high, b_low) + part(a_low, b_high))


def line(ref, f):
    return ref[pl.ds(f, K, stride=F), :]


def place(c, x, y):
    return (c * 4 + x) * 4 + y


def wide(ref):
    return jnp.concatenate([line(ref, f) for f in range(F)], axis=1)


def narrow(value, ref):
    for f in range(F):
        ref[pl.ds(f, K, stride=F), :] = value[:, f * LANES : (f + 1) * LANES]


def call(kernel, outs, fetched, stored, scratch=(), flops=10_000_000, unread=0, name=None, held=0):
    def run(*args):
        n, m = len(args), len(outs)
        whole = n - unread - fetched
        vmem, hbm = pl.BlockSpec(memory_space=pltpu.VMEM), pl.BlockSpec(memory_space=pltpu.HBM)

        def body(*refs):
            given, made, own = refs[:n], refs[n : n + m], refs[n + m :]
            buffers, semaphores = own[: fetched + stored], own[fetched + stored : 2 * (fetched + stored)]
            rest = own[2 * (fetched + stored) :]
            fetches = [
                pltpu.make_async_copy(*three) for three in zip(given[:fetched], buffers[:fetched], semaphores[:fetched])
            ]
            stores = [
                pltpu.make_async_copy(*three) for three in zip(buffers[fetched:], made[:stored], semaphores[fetched:])
            ]
            for fetch in fetches:
                fetch.start()
            kernel(
                lambda i: fetches[i].wait(),
                lambda i: stores[i].start(),
                *buffers[:fetched],
                *given[fetched : fetched + whole],
                *buffers[fetched:],
                *made[stored:],
                *rest,
            )
            for store in stores:
                store.wait()

        sizes = [a.size for a in args[: fetched + whole]]
        for o in outs:
            sizes.append(1)
            for length in o:
                sizes[-1] *= length
        return pl.pallas_call(
            body,
            out_shape=[pltpu.HBM(o, jnp.float32) for o in outs[:stored]]
            + [jax.ShapeDtypeStruct(o, jnp.float32) for o in outs[stored:]],
            in_specs=[hbm] * fetched + [vmem] * whole + [hbm] * unread,
            out_specs=[hbm] * stored + [vmem] * (m - stored),
            scratch_shapes=[pltpu.VMEM(a.shape, jnp.float32) for a in args[:fetched]]
            + [pltpu.VMEM(o, jnp.float32) for o in outs[:stored]]
            + [pltpu.SemaphoreType.DMA] * (fetched + stored)
            + [pltpu.VMEM(shape, jnp.float32) for shape in scratch],
            compiler_params=pltpu.CompilerParams(vmem_limit_bytes=24 * 1024 * 1024),
            cost_estimate=pl.CostEstimate(flops=flops, bytes_accessed=4 * sum(sizes), transcendentals=0),
            name=name,
            )(
            *(pltpu.with_memory_space_constraint(a, pltpu.HBM) for a in args[:fetched]),
            *(pltpu.with_memory_space_constraint(a, pltpu.VMEM) for a in args[fetched : fetched + held]),
            *args[fetched + held :],
        )

    return run


def slab_kernel(p_hbm, factor, low_x, high_x, low_y, high_y, blocks, p, whole, fetched, sent):
    fetch = pltpu.make_async_copy(p_hbm, p, fetched.at[4])
    fetch.start()
    parts = [
        pltpu.make_async_copy(
            factor.at[:, pl.ds(i * 2048, 2048)], whole.at[:, pl.ds(i * 2048, 2048)], fetched.at[i]
        )
        for i in range(4)
    ]
    for part in parts:
        part.start()
    cuts = [
        pltpu.make_async_copy(whole.at[:, pl.ds(g * 512, 512)], blocks.at[g], sent.at[g]) for g in range(16)
    ]
    for i, part in enumerate(parts):
        part.wait()
        for cut in cuts[4 * i : 4 * i + 4]:
            cut.start()
    fetch.wait()
    at = 0
    for c in range(3):
        for x in range(2):
            for y in range(4):
                low_x[pl.ds(at * K, K), :] = line(p, place(c, x, y))
                high_x[pl.ds(at * K, K), :] = line(p, place(c, x + 2, y))
                at += 1
    at = 0
    for c in range(3):
        for x in range(4):
            for y in range(2):
                low_y[pl.ds(at * K, K), :] = line(p, place(c, x, y))
                high_y[pl.ds(at * K, K), :] = line(p, place(c, x, y + 2))
                at += 1
    for cut in cuts:
        cut.wait()


def halo_slabs(p, factor):
    rows = p.shape[0]
    hbm, vmem = pl.BlockSpec(memory_space=pltpu.HBM), pl.BlockSpec(memory_space=pltpu.VMEM)
    return pl.pallas_call(
        slab_kernel,
        out_shape=[jax.ShapeDtypeStruct((rows // 2, LANES), jnp.float32)] * 4 + [pltpu.HBM((16, K, 512), jnp.float32)],
        in_specs=[hbm] * 2,
        out_specs=[vmem] * 4 + [hbm],
        scratch_shapes=[
            pltpu.VMEM(p.shape, jnp.float32),
            pltpu.VMEM(factor.shape, jnp.float32),
            pltpu.SemaphoreType.DMA((5,)),
            pltpu.SemaphoreType.DMA((16,)),
        ],
        compiler_params=pltpu.CompilerParams(vmem_limit_bytes=24 * 1024 * 1024),
        cost_estimate=pl.CostEstimate(flops=1_000_000, bytes_accessed=5_000_000, transcendentals=0),
        name="halo_slabs",
    )(*(pltpu.with_memory_space_constraint(a, pltpu.HBM) for a in (p, factor)))


def image_kernel(wait, put, p, mass, inverse, basis, r, below_x, below_y, above_y, above_x, q, sums, inner, left, right, lines):
    lane = lax.broadcasted_iota(jnp.int32, (K, LANES), 1)

    def at(c, x, y):
        if x < 0:
            return below_x[pl.ds(((c * 2 + x + 2) * 4 + y) * K, K), :]
        if x > 3:
            return above_x[pl.ds(((c * 2 + x - 4) * 4 + y) * K, K), :]
        if y < 0:
            return below_y[pl.ds(((c * 4 + x) * 2 + y + 2) * K, K), :]
        if y > 3:
            return above_y[pl.ds(((c * 4 + x) * 2 + y - 4) * K, K), :]
        return left[pl.ds(0, K), pl.ds(place(c, x, y) * LANES, LANES)]

    wait(0)
    for f in range(F):
        left[pl.ds(0, K), pl.ds(f * LANES, LANES)] = line(p, f)
    wait(1)
    for c in range(3):
        for x in range(4):
            for y in range(4):
                f = place(c, x, y)
                center = at(c, x, y)
                near = at(c, x - 1, y) + at(c, x + 1, y) + at(c, x, y - 1) + at(c, x, y + 1)
                far = at(c, x - 2, y) + at(c, x + 2, y) + at(c, x, y - 2) + at(c, x, y + 2)
                near = near + jnp.where(lane >= 1, pltpu.roll(center, 1, 1), 0.0)
                near = near + jnp.where(lane < LANES - 1, pltpu.roll(center, LANES - 1, 1), 0.0)
                far = far + jnp.where(lane >= 2, pltpu.roll(center, 2, 1), 0.0)
                far = far + jnp.where(lane < LANES - 2, pltpu.roll(center, LANES - 2, 1), 0.0)
                weight = mass[pl.ds(x * 4 + y, 1), :] + 7.5
                value = weight * center - (4.0 / 3.0) * near + (1.0 / 12.0) * far
                q[:, pl.ds(f * LANES, LANES)] = value
                right[pl.ds(0, K), pl.ds(f * LANES, LANES)] = value
                lines[pl.ds(f * K, K), :] = value
    put(0)
    wait(2)
    lines[...] = dot3(lines[...], inverse[...])
    wait(3)
    wait(4)
    for f in range(F):
        columns = pl.ds(f * LANES, LANES)
        left[pl.ds(K, K), columns] = line(basis, f)
        left[pl.ds(2 * K, K), columns] = lines[pl.ds(f * K, K), :]
        right[pl.ds(K, K), columns] = line(r, f)
    every = dot3(left[...], right[...], ((1,), (1,)))
    sums[...] = jnp.concatenate([every[:K], every[K : 2 * K]], axis=1)
    inner[...] = every[2 * K :]


def slots(axis):
    own = lax.axis_index(axis)
    return [lax.rem(own + 4 - d, 4) for d in range(4)]


def gather_y_kernel(wait, put, sums_0, sums_1, sums_2, sums_3, out, lines):
    total = jnp.zeros((K, 64), jnp.float32)
    for slot, arrived in zip(slots("y"), (sums_0, sums_1, sums_2, sums_3)):
        lines[pl.ds(pl.multiple_of(slot * K, K), K), :] = arrived[...]
        total = total + arrived[:, :64]
    out[pl.ds(0, 64), :] = jnp.concatenate([lines[pl.ds(0, 64), :][:, 64:], lines[pl.ds(64, 64), :][:, 64:]], axis=1)
    out[pl.ds(64, 16), :] = jnp.concatenate([total[:16], total[16:]], axis=1)


def mid_kernel(wait, put, factor, group_0, group_1, group_2, group_3, out, rhs):
    total = jnp.zeros((16, LANES), jnp.float32)
    for slot, arrived in zip(slots("x"), (group_0, group_1, group_2, group_3)):
        for y in range(4):
            piece = arrived[pl.ds((y % 2) * K, K), :][:, (y // 2) * 64 : (y // 2 + 1) * 64]
            rhs[pl.ds(pl.multiple_of((y * 4 + slot) * K, K), K), :] = piece
        total = total + arrived[pl.ds(64, 16), :]
    total = jnp.concatenate([total[:, :64], total[:, 64:]], axis=0)
    mid = dot3(rhs[...].T, factor[...].reshape(512, 512)).T
    for g in range(16):
        out[g] = jnp.concatenate([mid[g * K : (g + 1) * K], total], axis=1)


def packed4(a, b):
    return jnp.concatenate([a[:16], a[16:], b[:16], b[16:]], axis=1)


def alpha_kernel(wait, put, arrived, inner, alpha, gram_inverse, out):
    total = jnp.sum(arrived[...], axis=0)
    mid_q, mid_r = total[:, :32], total[:, 32:64]
    gram, proj = total[:, 64:96], total[:, 96:]
    base = inner[...] + dot3(mid_q, total[:, : 2 * K], ((0,), (0,)))
    row = lax.broadcasted_iota(jnp.int32, (K, K), 0)
    column = lax.broadcasted_iota(jnp.int32, (K, K), 1)
    work = jnp.concatenate([gram, (row == column).astype(jnp.float32), proj], axis=1)
    at = lax.broadcasted_iota(jnp.int32, (K, 1), 0)
    for j in range(0, K, 2):
        first, second = work[j : j + 1, :], work[j + 1 : j + 2, :]
        pivot = 1.0 / first[:, j : j + 1]
        scaled = first * pivot
        second = second - second[:, j : j + 1] * scaled
        second = second * (1.0 / second[:, j + 1 : j + 2])
        first = scaled - scaled[:, j + 1 : j + 2] * second
        rest = work - work[:, j : j + 1] * first - work[:, j + 1 : j + 2] * second
        work = jnp.where(at == j, first, jnp.where(at == j + 1, second, rest))
    mix = work[:, 2 * K :]
    inverse = work[:, K : 2 * K]
    alpha[...] = mix
    gram_inverse[...] = inverse
    after = dot3(jnp.concatenate([mid_q, base[:, :K]], axis=0), mix)
    coarse_mid = mid_r - after[:K]
    cross = base[:, K:] - after[K:]
    packed = packed4(coarse_mid, cross)
    for g in range(16):
        out[g] = packed


def sol_kernel(wait, put, factor, gathered, out):
    cross = jnp.sum(gathered[...], axis=0)[:, 64:]
    mid = jnp.concatenate([gathered[g][:, h : h + K] for g in range(16) for h in (0, K)], axis=0)
    sol = dot3(factor[...].reshape(512, 512), mid)
    for g in range(16):
        at = g * K
        out[g] = jnp.concatenate([sol[at : at + 16], sol[at + 16 : at + K], cross], axis=1)


def update_kernel(wait, put, q, r, inverse, s, p, basis, alpha, new_s, new_r, local, left, lines):
    mix = alpha[...]
    wait(0)
    wait(1)
    narrow(wide(r) - dot3(mix, q[...], ((0,), (0,))), new_r)
    put(1)
    wait(2)
    lines[...] = dot3(new_r[...], inverse[...], ((1,), (1,)))
    local[...] = wide(lines)
    wait(3)
    wait(4)
    wait(5)
    for f in range(F):
        columns = pl.ds(f * LANES, LANES)
        left[pl.ds(0, K), columns] = line(p, f)
        left[pl.ds(K, K), columns] = line(basis, f)
    narrow(wide(s) + dot3(mix, left[pl.ds(0, K), :], ((0,), (0,))), new_s)
    put(0)


def direction_kernel(wait, put, left, local, arrived, gram_inverse, new_p):
    total = jnp.sum(arrived[...], axis=0)
    sol = jnp.concatenate([total[:, :32], total[:, 32:64]], axis=0)
    cross = jnp.concatenate([total[:, 64:96], total[:, 96:]], axis=0)
    beta = -dot(gram_inverse[...], cross)
    mix = jnp.concatenate([beta, sol], axis=0)
    narrow(local[...] + dot3(mix, left[...], ((0,), (0,))), new_p)
    put(0)


def swapped(array, axes):
    return lax.all_to_all(array, axes, 0, 0, tiled=True)


def from_all(array, axis):
    n = lax.axis_size(axis)
    return [array] + [lax.ppermute(array, axis, [(i, (i + d) % n) for i in range(n)]) for d in range(1, n)]


def on_device(solution, residual, direction, mass, coarse_basis, line_inverse, coarse_factor):
    shape = direction.shape
    s, r, p, basis = (a.reshape(-1, LANES) for a in (solution, residual, direction, coarse_basis))
    inverse = line_inverse[0, 0]
    rows, length = p.shape
    flat = (K, F * LANES)

    double = (2 * K, F * LANES)
    low_x, high_x, low_y, high_y, blocks = halo_slabs(p, coarse_factor)
    up_sub = [(i, i + 1) for i in range(63)]
    up_inner = [(i, i + 1) for i in range(3)]
    below_x = lax.ppermute(high_x, SUB, up_sub)
    above_x = lax.ppermute(low_x, SUB, [(b, a) for a, b in up_sub])

    below_y = lax.ppermute(high_y, "x", up_inner)
    above_y = lax.ppermute(low_y, "x", [(b, a) for a, b in up_inner])
    factor = swapped(blocks, ROWS)
    q, sums, inner = call(
        image_kernel,
        [flat, (K, LANES), (K, 2 * K)],
        5,
        1,
        [(3 * K, F * LANES), double, (rows, LANES)],
        50_000_000_000,
        held=4,
        name="image",
    )(p, mass.reshape(16, LANES), inverse, basis, r, below_x, below_y, above_y, above_x)
    (group,) = call(gather_y_kernel, [(80, LANES)], 0, 0, [(4 * K, LANES)], name="gather_y")(*from_all(sums, "y"))
    (parts,) = call(mid_kernel, [(16, K, LANES)], 0, 0, [(512, 64)], held=1, name="coarse_mid")(
        factor, *from_all(group, "x")
    )
    arrived = swapped(parts, COLS)
    alpha, gram_inverse, spread = call(alpha_kernel, [(K, K), (K, K), (16, 16, LANES)], 0, 0, name="alpha")(
        arrived, inner
    )
    mids = swapped(spread, COLS)
    new_s, new_r, local, both = call(
        update_kernel, [(rows, LANES)] * 2 + [flat, double], 6, 2, [(rows, LANES)], 75_000_000, name="updates"
    )(q, r, inverse, s, p, basis, alpha)
    (sols,) = call(sol_kernel, [(16, 16, LANES)], 0, 0, held=1, name="coarse_sol")(factor, mids)
    last = swapped(sols, ROWS)
    (new_p,) = call(direction_kernel, [(rows, LANES)], 0, 1, flops=25_000_000, held=2, name="new_direction")(
        both, local, last, gram_inverse
    )
    return new_s.reshape(shape), new_r.reshape(shape), new_p.reshape(shape)


def solution(mesh):
    torus = Mesh(mesh.devices.reshape(8, 4, 2, 4), ("z", "y", "core", "x"))
    field = P(None, None, SUB, "x", None)
    return jax.shard_map(
        on_device,
        mesh=torus,
        in_specs=(field, field, field, P(SUB, "x", None), field, P(SUB, "x", None, None), P(SUB + ("x",), None)),
        out_specs=(field, field, field),
        check_vma=False,
    )
```
